128 devices in a mesh: rep: 4 (over y_hi, core), fsdp: 32 (over x, z, y_lo).
Axes of the slice: x: 4, y: 4 (y_hi: 2, y_lo: 2; y = y_hi * 2 + y_lo), z: 4, core: 2. Of those that a mesh axis runs over, the one named last changes fastest.
Arguments:
- tokens: bfloat16 [98304, 4096], P(('rep', 'fsdp')), may hold values from -6 to 6
- cotangent: bfloat16 [98304, 1024], P(('rep', 'fsdp')), may hold values from -6 to 6
- weight: float32 [4096, 1024], P('fsdp'), may hold values from -0.09375 to 0.09375
- momentum: float32 [4, 4096, 1024], P('rep', 'fsdp'), may hold values from -6 to 6
- kept: int32 [4, 64, 16, 2], P(None, 'fsdp'), may hold values from 0 to 63, all different within a row
Outputs:
- input_grad: bfloat16 [98304, 4096], P(('rep', 'fsdp'))
- new_momentum: float32 [4, 4096, 1024], P('rep', 'fsdp')
- new_weight: float32 [4096, 1024], P('fsdp')
- update: float32 [4096, 1024], P('fsdp')
The draws below stay inside these ranges and needn't reach their ends.
Inputs may be any that keep to these rules, and one draw needn't show every extreme that they name: `kept`: each row of the last dimension names 2 different block numbers.
All inputs are finite; a program needn't handle non-finite values.
Results may differ from the reference program's by a relative error of at most 0.0049.
Values may be sent and summed in bfloat16 or wider, within the bound.
A program may use at most 128 MiB of HBM per device.

```python
import jax
import jax.numpy as jnp
from jax import lax

D = 4096
KV = 1024
TOK_DEV = 768
TILE = 64
BLK = 8
K = 2
REPS = 4
TOKENS = 98304
N_REP = 4
N_FSDP = 32


def block_levels(rng, extent, pieces, low, largest):
    level, own = 1.0, jax.random.fold_in(rng, 6)
    for axis_at, shards_of in pieces:
        steps = jnp.exp(jax.random.uniform(jax.random.fold_in(own, axis_at), (shards_of,), jnp.float32, low / len(pieces), largest / len(pieces)))
        level = level * jnp.repeat(steps, extent[axis_at] // shards_of).reshape([-1 if axis == axis_at else 1 for axis in range(len(extent))])
    return level


def choose_distinct(rng, rows, count, top, lift):
    ranking = jax.random.permutation(jax.random.fold_in(rng, 1), count)
    favour = ranking
    for power in range(3):
        favour = favour * favour // count
    favour = favour * lift // count
    tickets = jax.random.randint(jax.random.fold_in(rng, 2), (rows, count), 0, 4096) + favour
    fixed_rows = jax.random.permutation(jax.random.fold_in(rng, 3), rows)[jnp.arange(count) % rows]
    tickets = jnp.where(jnp.arange(rows)[:, None] == fixed_rows[None, :], 1 << 14, tickets)
    score = tickets * count + jnp.arange(count)
    return lax.top_k(score.astype(jnp.int32), top)[1].astype(jnp.int32)


def noise(rng, extent, deviation, most, pieces=(), kind=jnp.bfloat16):
    values = deviation * jax.random.normal(rng, extent, jnp.float32)
    if pieces:
        values = values * block_levels(rng, extent, pieces, -0.22, 0.18)
    return jnp.clip(values, -most, most).astype(kind)


def setup_inputs(seed: int = 0) -> dict:
    key_list = jax.random.split(jax.random.key(seed), 6)
    tokens = noise(key_list[0], (TOKENS, D), 1.0, 6.0, ((0, 128),))
    cotangent = noise(key_list[1], (TOKENS, KV), 1.0, 6.0, ((0, 128),))
    weight = noise(key_list[2], (D, KV), D ** -0.5, 0.09375, ((0, 32),), jnp.float32)
    momentum = noise(key_list[3], (REPS, D, KV), 1.0, 6.0, ((0, 4), (1, 32)), jnp.float32)
    kept = choose_distinct(key_list[4], REPS * (D // TILE) * (KV // TILE), (TILE // BLK) * (TILE // BLK), K, 0).reshape((REPS, D // TILE, KV // TILE, K))
    return {"tokens": tokens, "cotangent": cotangent, "weight": weight, "momentum": momentum, "kept": kept}


decay_rate = 0.999
step_size = 0.02
highest = lax.Precision.HIGHEST

def dct_table():
    freq = jnp.arange(TILE, dtype=jnp.float32)[:, None]
    place = jnp.arange(TILE, dtype=jnp.float32)[None, :]
    table = jnp.cos(jnp.pi * (2.0 * place + 1.0) * freq / (2.0 * TILE))
    norms = jnp.where(freq == 0.0, jnp.sqrt(1.0 / TILE), jnp.sqrt(2.0 / TILE))
    return table * norms

def to_tiles(field):
    height, width = field.shape
    return field.reshape(height // TILE, TILE, width // TILE, TILE).transpose(0, 2, 1, 3)

def from_tiles(tiles):
    rows_t, cols_t = (tiles.shape[0], tiles.shape[1])
    return tiles.transpose(0, 2, 1, 3).reshape(rows_t * TILE, cols_t * TILE)

def forward_dct(tiles, table):
    return jnp.einsum('ij,abjk,lk->abil', table, tiles, table, precision=highest)

def inverse_dct(coefs, table):
    return jnp.einsum('ji,abjk,kl->abil', table, coefs, table, precision=highest)

def to_blocks(coefs):
    side = TILE // BLK
    rows_t, cols_t = (coefs.shape[0], coefs.shape[1])
    split = coefs.reshape(rows_t, cols_t, side, BLK, side, BLK).transpose(0, 1, 2, 4, 3, 5)
    return split.reshape(rows_t, cols_t, side * side, BLK * BLK)

def from_blocks(blocks):
    side = TILE // BLK
    rows_t, cols_t = (blocks.shape[0], blocks.shape[1])
    split = blocks.reshape(rows_t, cols_t, side, side, BLK, BLK).transpose(0, 1, 2, 4, 3, 5)
    return split.reshape(rows_t, cols_t, TILE, TILE)

def selector(kept):
    side = TILE // BLK
    return (kept[..., None] == jnp.arange(side * side, dtype=jnp.int32)).astype(jnp.float32)

def reference(tokens, cotangent, weight, momentum, kept):
    table = dct_table()
    weight_b = weight.astype(jnp.bfloat16)
    input_grad = jnp.dot(cotangent, weight_b.T, preferred_element_type=jnp.float32).astype(jnp.bfloat16)
    new_moments = []
    total = None
    for replica in range(N_REP):

        def add_device(carry, device):
            start = (replica * N_FSDP + device) * TOK_DEV
            rows_x = lax.dynamic_slice_in_dim(tokens, start, TOK_DEV, 0)
            rows_g = lax.dynamic_slice_in_dim(cotangent, start, TOK_DEV, 0)
            term = jnp.dot(rows_x.T, rows_g, preferred_element_type=jnp.float32)
            return (carry + term, None)
        summed, _ = lax.scan(add_device, jnp.zeros((D, KV), jnp.float32), jnp.arange(N_FSDP, dtype=jnp.int32))
        gradient = summed / jnp.sqrt(jnp.float32(TOK_DEV * N_FSDP))
        current = decay_rate * momentum[replica] + gradient
        coefs = forward_dct(to_tiles(current), table)
        mask = selector(kept[replica])
        compact = jnp.einsum('abkn,abnc->abkc', mask, to_blocks(coefs), precision=highest)
        dense = jnp.einsum('abkn,abkc->abnc', mask, compact, precision=highest)
        sent = from_tiles(inverse_dct(from_blocks(dense), table))
        new_moments.append(current - sent)
        total = dense if total is None else total + dense
    average = inverse_dct(from_blocks(total), table) / N_REP
    spread = jnp.sqrt(lax.optimization_barrier(jnp.mean(average * average, axis=(2, 3), keepdims=True)) + 1e-06)
    update = from_tiles(average / (jnp.abs(average) + spread))
    new_weight = weight - step_size * update
    return (input_grad, jnp.stack(new_moments), new_weight, update)
```

```python
import functools

import jax
import jax.numpy as jnp
import numpy as np
from jax import lax
from jax.experimental import pallas as pl
from jax.experimental.pallas import tpu as pltpu
from jax.sharding import PartitionSpec as P

TILE = 64
BLK = 8
DECAY = 0.999
STEP = 0.02
HIGHEST = lax.Precision.HIGHEST
MESH = pl.DeviceIdType.MESH
F32 = jnp.float32
BF16 = jnp.bfloat16

PIECES = (("yxz", 0, 256), ("yzx", 256, 128), ("xyz", 384, 256), ("zyx", 640, 384))
OFFS = (2, 1, 3, 0)


def dct_matrix():
    freq = np.arange(TILE, dtype=np.float64)[:, None]
    place = np.arange(TILE, dtype=np.float64)[None, :]
    table = np.cos(np.pi * (2.0 * place + 1.0) * freq / (2.0 * TILE))
    table *= np.where(freq == 0.0, np.sqrt(1.0 / TILE), np.sqrt(2.0 / TILE))
    return np.kron(np.eye(2), table).astype(np.float32)


def fold_matrix():
    fold = np.zeros((1024, 128), np.float32)
    lane = np.arange(1024)
    fold[lane, (lane // TILE) * BLK + lane % BLK] = 1.0
    return fold


def dot(a, b, dims=(((1,), (0,)), ((), ()))):
    return lax.dot_general(a, b, dims, precision=HIGHEST, preferred_element_type=F32)


def tile_transform(field, left, right):
    mid = dot(left, field)
    return jnp.concatenate([dot(mid[:, i * 128 : (i + 1) * 128], right) for i in range(8)], axis=1)


def kept_lanes(kept):
    tile_of = lax.broadcasted_iota(jnp.int32, (16, 1024), 1) // TILE
    here = tile_of == lax.broadcasted_iota(jnp.int32, (16, 1024), 0)
    found = []
    for which in range(2):
        rows = []
        for a in range(2):
            numbers = kept[a][:, which : which + 1]
            spread = jnp.where(here, jnp.broadcast_to(numbers, (16, 1024)), 0)
            rows.append(jnp.sum(spread, axis=0, keepdims=True))
        found.append(rows)
    return found


def kept_masks(kept):
    number = lax.broadcasted_iota(jnp.int32, (8, 8, 1024), 0) * 8 + (
        lax.broadcasted_iota(jnp.int32, (8, 8, 1024), 2) % TILE
    ) // BLK
    masks = []
    for rows in kept_lanes(kept):
        masks.append(
            [number == jnp.broadcast_to(row.reshape(1, 1, 1024), (8, 8, 1024)) for row in rows]
        )
    return masks


def make_places():
    rep, shard = lax.axis_index("rep"), lax.axis_index("fsdp")
    yhi, core = rep // 2, rep % 2
    x, z, ylo = shard // 8, (shard // 2) % 4, shard % 2

    def at(yhi_=None, core_=None, x_=None, z_=None, ylo_=None):
        h = yhi if yhi_ is None else yhi_
        c = core if core_ is None else core_
        xx = x if x_ is None else x_
        zz = z if z_ is None else z_
        l = ylo if ylo_ is None else ylo_
        return (h * 2 + c, (xx * 4 + zz) * 2 + l)

    return yhi, core, x, z, ylo, at


def main_kernel(
    tok_hbm, cot_hbm, w_hbm, mom_hbm, kept_ref, dct_ref, fold_ref,
    ig_hbm, newmom_ref, ex_ref,
    tok, cot, w, mom, wf, p0, p1, p2, p3, a0, a1, a2, a3, b0, b1, b2, b3, c0, c1, c2, c3,
    ig, cur, local_sem, ig_sem, send_sem, recv_sem,
):
    yhi, core, x, z, ylo, at = make_places()
    oy = 1 - ylo
    parts, r1, r2, r3 = (p0, p1, p2, p3), (a0, a1, a2, a3), (b0, b1, b2, b3), (c0, c1, c2, c3)
    xk = [lax.rem(x + o, 4) for o in OFFS]
    zo = [lax.rem(z + o, 4) for o in (2, 1, 3)]
    x_peer = [at(x_=xk[k]) for k in range(3)]
    z_peer = [at(z_=zo[i]) for i in range(3)]
    y_peer = at(ylo_=oy)
    y_far = at(yhi_=1 - yhi, ylo_=oy)
    core_peer = at(core_=1 - core)
    rep_peers = [core_peer, at(yhi_=1 - yhi), at(yhi_=1 - yhi, core_=1 - core)]

    w_load = pltpu.make_async_copy(w_hbm, w, local_sem.at[0])
    cot_load = pltpu.make_async_copy(cot_hbm, cot, local_sem.at[1])
    mom_load = pltpu.make_async_copy(mom_hbm.at[0], mom, local_sem.at[2])
    tok_loads = []
    for k in range(4):
        cols = pl.ds(pl.multiple_of(xk[k] * 1024, 1024), 1024)
        tok_loads.append(pltpu.make_async_copy(tok_hbm.at[:, cols], tok.at[:, cols], local_sem.at[3 + k]))
    w_load.start()
    cot_load.start()
    for load in tok_loads:
        load.start()
    mom_load.start()

    barrier = pltpu.get_barrier_semaphore()
    everyone = x_peer + z_peer + [y_peer, y_far] + rep_peers
    for peer in everyone:
        pl.semaphore_signal(barrier, inc=1, device_id=peer, device_id_type=MESH)

    used = [0]
    sent = []

    def send(src, dst, peer):
        n = used[0]
        used[0] += 1
        copy = pltpu.make_async_remote_copy(
            src_ref=src, dst_ref=dst, send_sem=send_sem.at[n], recv_sem=recv_sem.at[n],
            device_id=peer, device_id_type=MESH,
        )
        copy.start()
        sent.append(copy)
        return copy

    def same(view, peer):
        return send(view, view, peer)

    w_load.wait()
    half = pl.multiple_of(core * 64, 64)
    wf[x, z, ylo, pl.ds(half, 64)] = w[pl.ds(half, 64), :].astype(BF16)
    pl.semaphore_wait(barrier, len(everyone))
    rows_x, rows_z = pl.ds(half, 32), pl.ds(pl.multiple_of(half + 32, 32), 32)
    rows_c = pl.ds(half, 64)
    gx = [same(wf.at[x, z, ylo, rows_x], peer) for peer in x_peer]
    gz = [same(wf.at[x, z, ylo, rows_z], peer) for peer in z_peer]

    cot_load.wait()
    s1 = [[] for _ in PIECES]
    for k in range(4):
        xs = xk[k]
        tok_loads[k].wait()

        def block(zz, carry, xs=xs):
            cols = pl.ds(pl.multiple_of((xs * 4 + zz) * 256, 256), 256)
            part = lax.dot_general(
                tok[:, cols], cot[...], (((0,), (0,)), ((), ())), preferred_element_type=F32
            ).astype(BF16)
            for ref, (_, lo, width) in zip(parts, PIECES):
                ref[xs, zz, 0] = part[:128, lo : lo + width]
                ref[xs, zz, 1] = part[128:, lo : lo + width]
            return carry

        lax.fori_loop(0, 4, block, 0)
        for i, (order, _, _) in enumerate(PIECES):
            if order[0] == "y":
                s1[i].append(send(parts[i].at[xs, :, oy], r1[i].at[xs], y_peer))
            elif order[0] == "x":
                if k < 3:
                    s1[i].append(send(parts[i].at[xs], r1[i].at[k], x_peer[k]))
            else:
                s1[i].append(
                    [send(parts[i].at[xs, zo[j]], r1[i].at[xs, j], z_peer[j]) for j in range(3)]
                )
        if k == 1:
            for copy in gx + gz:
                copy.wait_recv()
            hx = [same(wf.at[:, z, ylo, rows_x], peer) for peer in z_peer]
            hz = [same(wf.at[x, :, ylo, rows_z], peer) for peer in x_peer]

    for copy in hx + hz:
        copy.wait_recv()
    far = same(wf.at[:, :, ylo, rows_c], y_far)
    near = same(wf.at[:, :, ylo, rows_c], core_peer)

    def add_into(ref, sources, count):
        def one(i, carry):
            total = ref(i)[...].astype(F32)
            for source in sources:
                total += source(i)[...].astype(F32)
            ref(i)[...] = total.astype(BF16)
            return carry

        lax.fori_loop(0, count, one, 0)

    def input_grad(plane, base):
        def one(i, carry):
            xx, zz = i // 2, (i % 2) * 2
            rows = jnp.concatenate([wf[xx, zz, plane], wf[xx, zz + 1, plane]], axis=0)
            out = lax.dot_general(
                cot[...], rows, (((1,), (1,)), ((), ())), preferred_element_type=F32
            ).astype(BF16)
            ig[base + i, 0] = out[:, :128]
            ig[base + i, 1] = out[:, 128:]
            for j in range(2):
                cols = pl.ds(pl.multiple_of(((xx * 4 + zz + j) * 2 + plane) * 128, 128), 128)
                pltpu.make_async_copy(ig.at[base + i, j], ig_hbm.at[:, cols], ig_sem.at[base + i, j]).start()
            return carry

        lax.fori_loop(0, 8, one, 0)

    near.wait_recv()
    input_grad(ylo, 0)

    s2 = [[] for _ in PIECES]
    for k in range(4):
        xs = xk[k]
        for i, (order, _, _) in enumerate(PIECES):
            if order[0] == "y":
                s1[i][k].wait_recv()
                add_into(
                    lambda c, i=i, xs=xs: parts[i].at[xs, c, ylo],
                    [lambda c, i=i, xs=xs: r1[i].at[xs, c]], 4,
                )
                if order == "yxz":
                    if k < 3:
                        s2[i].append(send(parts[i].at[xs, :, ylo], r2[i].at[k], x_peer[k]))
                else:
                    s2[i].append(
                        [send(parts[i].at[xs, zo[j], ylo], r2[i].at[xs, j], z_peer[j]) for j in range(3)]
                    )
            elif order == "zyx":
                for copy in s1[i][k]:
                    copy.wait_recv()
                add_into(
                    lambda c, i=i, xs=xs: parts[i].at[xs, z, c],
                    [lambda c, i=i, xs=xs, j=j: r1[i].at[xs, j, c] for j in range(3)], 2,
                )
                s2[i].append(send(parts[i].at[xs, z, oy], r2[i].at[xs], y_peer))
    for i, (order, _, _) in enumerate(PIECES):
        if order == "xyz":
            for copy in s1[i]:
                copy.wait_recv()
            add_into(
                lambda c, i=i: parts[i].at[x, c // 2, c % 2],
                [lambda c, i=i, j=j: r1[i].at[j, c // 2, c % 2] for j in range(3)], 8,
            )
            s2[i].append(send(parts[i].at[x, :, oy], r2[i].at[...], y_peer))

    s3 = [[] for _ in PIECES]
    for i, (order, _, _) in enumerate(PIECES):
        if order == "yxz" or order == "xyz":
            for copy in s2[i]:
                copy.wait_recv()
            if order == "yxz":
                sources = [lambda c, i=i, j=j: r2[i].at[j, c] for j in range(3)]
            else:
                sources = [lambda c, i=i: r2[i].at[c]]
            add_into(lambda c, i=i: parts[i].at[x, c, ylo], sources, 4)
            for j in range(3):
                s3[i].append(send(parts[i].at[x, zo[j], ylo], r3[i].at[j], z_peer[j]))
        else:
            for k in range(4):
                xs = xk[k]
                for copy in s2[i][k] if order == "yzx" else [s2[i][k]]:
                    copy.wait_recv()
                if order == "yzx":
                    sources = [lambda c, i=i, xs=xs, j=j: r2[i].at[xs, j] for j in range(3)]
                else:
                    sources = [lambda c, i=i, xs=xs: r2[i].at[xs]]
                add_into(lambda c, i=i, xs=xs: parts[i].at[xs, z, ylo], sources, 1)
                if k < 3:
                    s3[i].append(send(parts[i].at[xs, z, ylo], r3[i].at[k], x_peer[k]))

    far.wait_recv()
    near2 = same(wf.at[:, :, oy, rows_c], core_peer)
    near2.wait_recv()
    input_grad(oy, 8)

    mom_load.wait()
    for i, (_, lo, width) in enumerate(PIECES):
        for copy in s3[i]:
            copy.wait_recv()
        total = parts[i][x, z, ylo].astype(F32)
        for j in range(3):
            total += r3[i][j].astype(F32)
        cur[:, lo : lo + width] = DECAY * mom[:, lo : lo + width] + total * (1.0 / np.sqrt(24576.0))
    table = dct_ref[...]
    current = cur[...]
    coefs = tile_transform(current, table, table.T).reshape(2, 8, 8, 1024)
    me = lax.axis_index("rep")
    masks = kept_masks([kept_ref[me, a] for a in range(2)])
    folded, dense = [], []
    for which in range(2):
        for a in range(2):
            folded.append(jnp.sum(jnp.where(masks[which][a], coefs[a], 0.0), axis=0))
    for a in range(2):
        dense.append(jnp.where(masks[0][a] | masks[1][a], coefs[a], 0.0).reshape(64, 1024))
    ex_ref[me] = dot(jnp.concatenate(folded, axis=0), fold_ref[...])
    shared = [same(ex_ref.at[me], peer) for peer in rep_peers]
    newmom_ref[0] = current - tile_transform(jnp.concatenate(dense, axis=0), table.T, table)
    for copy in shared:
        copy.wait_recv()
    for copy in sent:
        copy.wait_send()

    def drain(i, carry):
        for j in range(2):
            pltpu.make_async_copy(ig.at[i, j], ig_hbm.at[:, pl.ds(0, 128)], ig_sem.at[i, j]).wait()
        return carry

    lax.fori_loop(0, 16, drain, 0)


def last_kernel(
    ig_in, mom_in, ex_ref, kept_ref, w_ref, dct_ref, fold_ref, ones_ref,
    ig_out, mom_out, neww_ref, upd_ref, sem,
):
    ig_copy = pltpu.make_async_copy(ig_in, ig_out, sem.at[0])
    mom_copy = pltpu.make_async_copy(mom_in, mom_out, sem.at[1])
    ig_copy.start()
    mom_copy.start()
    table = dct_ref[...]
    total = [jnp.zeros((8, 8, 1024), F32)] * 2
    spread_dims = (((1,), (1,)), ((), ()))
    wide = dot(ex_ref[...].reshape(128, 128), fold_ref[...], spread_dims).reshape(4, 2, 2, 8, 1024)
    for r in range(4):
        masks = kept_masks([kept_ref[r, a] for a in range(2)])
        for a in range(2):
            first = jnp.broadcast_to(wide[r, 0, a][None], (8, 8, 1024))
            second = jnp.broadcast_to(wide[r, 1, a][None], (8, 8, 1024))
            total[a] += jnp.where(masks[0][a], first, jnp.where(masks[1][a], second, 0.0))
    field = jnp.concatenate([t.reshape(64, 1024) for t in total], axis=0)
    average = tile_transform(field, table.T, table) * 0.25
    squares = jnp.sum((average * average).reshape(2, 64, 1024), axis=1)
    stacked = jnp.concatenate([squares[:, i * 128 : (i + 1) * 128] for i in range(8)], axis=0)
    means = dot(stacked, ones_ref[...]) * (1.0 / (TILE * TILE))
    spread = jnp.sqrt(means + 1e-06)
    for i in range(8):
        for a in range(2):
            rows, cols = slice(a * 64, a * 64 + 64), slice(i * 128, i * 128 + 128)
            avg = average[rows, cols]
            update = avg / (jnp.abs(avg) + spread[i * 2 + a : i * 2 + a + 1])
            upd_ref[rows, cols] = update
            neww_ref[rows, cols] = w_ref[rows, cols] - STEP * update
    ig_copy.wait()
    mom_copy.wait()


def body(tokens, cotangent, weight, momentum, kept):
    any_space = pl.BlockSpec(memory_space=pl.ANY)
    vmem = pl.BlockSpec(memory_space=pltpu.VMEM)
    first, second, third = [], [], []
    for order, _, width in PIECES:
        if order[0] == "y":
            first.append((4, 4, 128, width))
            second.append((3, 4, 128, width) if order == "yxz" else (4, 3, 128, width))
        elif order[0] == "x":
            first.append((3, 4, 2, 128, width))
            second.append((4, 128, width))
        else:
            first.append((4, 3, 2, 128, width))
            second.append((4, 128, width))
        third.append((3, 128, width))
    table, fold = jnp.asarray(dct_matrix()), jnp.asarray(fold_matrix())
    ones = jnp.asarray(np.kron(np.eye(2), np.ones((TILE, TILE))).astype(np.float32))
    sems = 96
    ig, newmom, shared = pl.pallas_call(
        main_kernel,
        out_shape=(
            jax.ShapeDtypeStruct((768, 4096), BF16),
            jax.ShapeDtypeStruct((1, 128, 1024), F32),
            jax.ShapeDtypeStruct((4, 32, 128), F32),
        ),
        in_specs=[any_space] * 4 + [vmem] * 3,
        out_specs=(any_space, vmem, vmem),
        scratch_shapes=[
            pltpu.VMEM((768, 4096), BF16),
            pltpu.VMEM((768, 1024), BF16),
            pltpu.VMEM((128, 1024), F32),
            pltpu.VMEM((128, 1024), F32),
            pltpu.VMEM((4, 4, 2, 128, 1024), BF16),
        ]
        + [pltpu.VMEM((4, 4, 2, 128, width), BF16) for _, _, width in PIECES]
        + [pltpu.VMEM(shape, BF16) for shape in first + second + third]
        + [
            pltpu.VMEM((16, 2, 768, 128), BF16),
            pltpu.VMEM((128, 1024), F32),
            pltpu.SemaphoreType.DMA((8,)),
            pltpu.SemaphoreType.DMA((16, 2)),
            pltpu.SemaphoreType.DMA((sems,)),
            pltpu.SemaphoreType.DMA((sems,)),
        ],
        compiler_params=pltpu.CompilerParams(
            collective_id=0, has_side_effects=True, vmem_limit_bytes=60 << 20
        ),
        cost_estimate=pl.CostEstimate(flops=13 * 10**9, bytes_accessed=20 * 10**6, transcendentals=0),
        name="gradients",
    )(tokens, cotangent, weight, momentum, kept, table, fold)
    return pl.pallas_call(
        last_kernel,
        out_shape=(
            jax.ShapeDtypeStruct((768, 4096), BF16),
            jax.ShapeDtypeStruct((1, 128, 1024), F32),
            jax.ShapeDtypeStruct((128, 1024), F32),
            jax.ShapeDtypeStruct((128, 1024), F32),
        ),
        in_specs=[any_space] * 2 + [vmem] * 6,
        out_specs=(any_space, any_space, vmem, vmem),
        scratch_shapes=[pltpu.SemaphoreType.DMA((2,))],
        compiler_params=pltpu.CompilerParams(vmem_limit_bytes=40 << 20),
        name="step",
    )(ig, newmom, shared, kept, weight, table, fold, ones)


def solution(mesh):
    in_specs = (
        P(("rep", "fsdp"), None),
        P(("rep", "fsdp"), None),
        P("fsdp", None),
        P("rep", "fsdp", None),
        P(None, "fsdp", None, None),
    )
    out_specs = (P(("rep", "fsdp"), None), P("rep", "fsdp", None), P("fsdp", None), P("fsdp", None))
    return jax.shard_map(body, mesh=mesh, in_specs=in_specs, out_specs=out_specs, check_vma=False)
```

```python
import jax
import jax.numpy as jnp
import numpy as np
from jax import lax
from jax.experimental import pallas as pl
from jax.experimental.pallas import tpu as pltpu
from jax.sharding import PartitionSpec as P

TILE = 64
BLK = 8
DECAY = 0.999
STEP = 0.02
MESH = pl.DeviceIdType.MESH
F32 = jnp.float32
BF16 = jnp.bfloat16

WIDTH = 128
Y_PIECES, X_PIECES, Z_PIECES = (0, 1), (2, 3, 4), (5, 6, 7)
OFFS = (2, 1, 3, 0)


def dct_matrix(copies):
    freq = np.arange(TILE, dtype=np.float64)[:, None]
    place = np.arange(TILE, dtype=np.float64)[None, :]
    table = np.cos(np.pi * (2.0 * place + 1.0) * freq / (2.0 * TILE))
    table *= np.where(freq == 0.0, np.sqrt(1.0 / TILE), np.sqrt(2.0 / TILE))
    return np.kron(np.eye(copies), table).astype(np.float32)


def two_halves(matrix):
    high = matrix.astype(jnp.bfloat16)
    low = (matrix - high.astype(np.float32)).astype(jnp.bfloat16)
    return np.stack([high, low])


def fold_matrix():
    fold = np.zeros((1024, 128), np.float32)
    lane = np.arange(1024)
    fold[lane, (lane // TILE) * BLK + lane % BLK] = 1.0
    return fold.astype(jnp.bfloat16)


def tile_lanes():
    return (np.arange(16)[:, None] == np.arange(1024)[None, :] // TILE).astype(jnp.bfloat16)


PLAIN = (((1,), (0,)), ((), ()))
TURNED = (((1,), (1,)), ((), ()))
FROM_LEFT = (((0,), (0,)), ((), ()))


def dot(a, b, dims=PLAIN):
    return lax.dot_general(a, b, dims, preferred_element_type=F32)


def halves(a):
    high = a.astype(BF16)
    return high, (a - high.astype(F32)).astype(BF16)


def dot_wide(a, b, dims=PLAIN):
    return dot(a[0], b[0], dims) + (dot(a[0], b[1], dims) + dot(a[1], b[0], dims))


def dot_exact(a, marks, dims=PLAIN):
    high, rest = a.astype(BF16), a
    rest = a - high.astype(F32)
    mid = rest.astype(BF16)
    low = (rest - mid.astype(F32)).astype(BF16)
    return dot(high, marks, dims) + (dot(mid, marks, dims) + dot(low, marks, dims))


def to_coefs(field, rows, lanes):
    mid = halves(dot_wide(rows, halves(field)))
    return jnp.concatenate(
        [dot_wide([m[:, i * 256 : i * 256 + 256] for m in mid], lanes, TURNED) for i in range(4)], axis=1
    )


def from_coefs(coefs, rows, lanes):
    mid = halves(dot_wide(rows, halves(coefs), FROM_LEFT))
    return jnp.concatenate(
        [dot_wide([m[:, i * 256 : i * 256 + 256] for m in mid], lanes) for i in range(4)], axis=1
    )


def kept_masks(kept, tile_lane):
    number = lax.broadcasted_iota(jnp.int32, (8, 8, 1024), 0) * 8 + (
        lax.broadcasted_iota(jnp.int32, (8, 8, 1024), 2) % TILE
    ) // BLK
    number = number.astype(F32)
    masks = [[], []]
    for rows in kept:
        spread = dot(rows.astype(F32).astype(BF16), tile_lane)
        for which in range(2):
            row = spread[which : which + 1].reshape(1, 1, 1024)
            masks[which].append(number == jnp.broadcast_to(row, (8, 8, 1024)))
    return masks


def make_places():
    rep, shard = lax.axis_index("rep"), lax.axis_index("fsdp")
    yhi, core = rep // 2, rep % 2
    x, z, ylo = shard // 8, (shard // 2) % 4, shard % 2

    def at(yhi_=None, core_=None, x_=None, z_=None, ylo_=None):
        h = yhi if yhi_ is None else yhi_
        c = core if core_ is None else core_
        xx = x if x_ is None else x_
        zz = z if z_ is None else z_
        l = ylo if ylo_ is None else ylo_
        return (h * 2 + c, (xx * 4 + zz) * 2 + l)

    return yhi, core, x, z, ylo, at


def main_kernel(
    tok_hbm, cot_hbm, w_hbm, mom_hbm, kept_hbm, rows_hbm, lanes_hbm, fold_hbm, tile_hbm,
    ig_hbm, newmom_hbm, ex_hbm,
    tok, cot, w, mom, kept_ref, rows_ref, lanes_ref, fold_ref, tile_ref,
    wf, parts, got_y, got_s1, got_x2, got_z2, got_y2, got_last,
    ig, cur, newmom, ex, local_sem, ig_sem, send_sem, recv_sem,
):
    yhi, core, x, z, ylo, at = make_places()
    oy = 1 - ylo
    xk = [lax.rem(x + o, 4) for o in OFFS]
    zk = [lax.rem(z + o, 4) for o in OFFS]
    x_peer = [at(x_=xk[k]) for k in range(3)]
    z_peer = [at(z_=zk[k]) for k in range(3)]
    y_peer = at(ylo_=oy)
    y_far = at(yhi_=1 - yhi, ylo_=oy)
    core_peer = at(core_=1 - core)
    rep_peers = [at(yhi_=1 - yhi), at(yhi_=1 - yhi, core_=1 - core), core_peer]

    w_load = pltpu.make_async_copy(w_hbm, w, local_sem.at[0])
    cot_load = pltpu.make_async_copy(cot_hbm, cot, local_sem.at[1])
    mom_load = pltpu.make_async_copy(mom_hbm.at[0], mom, local_sem.at[2])
    tok_loads = []
    for k in range(4):
        cols = pl.ds(pl.multiple_of(xk[k] * 1024, 1024), 1024)
        tok_loads.append(pltpu.make_async_copy(tok_hbm.at[:, cols], tok.at[:, cols], local_sem.at[3 + k]))
    w_load.start()
    cot_load.start()
    for load in tok_loads:
        load.start()
    mom_load.start()
    small = [(kept_hbm, kept_ref), (rows_hbm, rows_ref), (lanes_hbm, lanes_ref), (fold_hbm, fold_ref), (tile_hbm, tile_ref)]
    small = [pltpu.make_async_copy(src, dst, local_sem.at[7 + i]) for i, (src, dst) in enumerate(small)]
    for load in small:
        load.start()

    barrier = pltpu.get_barrier_semaphore()
    everyone = x_peer + z_peer + [y_peer, y_far] + rep_peers
    for peer in everyone:
        pl.semaphore_signal(barrier, inc=1, device_id=peer, device_id_type=MESH)

    used = [0]
    sent = []

    def send(src, dst, peer, tag="rs"):
        n = used[0]
        used[0] += 1
        copy = pltpu.make_async_remote_copy(
            src_ref=src, dst_ref=dst, send_sem=send_sem.at[n], recv_sem=recv_sem.at[n],
            device_id=peer, device_id_type=MESH,
        )
        copy.start()
        sent.append(copy)
        return copy

    def same(view, peer, tag="ag"):
        return send(view, view, peer, tag)

    w_load.wait()
    half = pl.multiple_of(core * 64, 64)
    rows_x, rows_z = pl.ds(half, 32), pl.ds(pl.multiple_of(half + 32, 32), 32)
    rows_c = pl.ds(half, 64)
    wf[x, z, ylo, rows_c] = w[rows_c, :].astype(BF16)
    pl.semaphore_wait(barrier, len(everyone))
    gx = [same(wf.at[x, z, ylo, rows_x], peer) for peer in x_peer]
    gz = [same(wf.at[x, z, ylo, rows_z], peer) for peer in z_peer]
    far = [(same(wf.at[x, z, ylo, rows_c], y_far, "far"), wf.at[x, z, oy, rows_c])]

    cot_load.wait()
    y1 = []
    for k in range(4):
        xs = xk[k]
        tok_loads[k].wait()

        def block(zz, carry, xs=xs):
            cols = pl.ds(pl.multiple_of((xs * 4 + zz) * 256, 256), 256)
            part = lax.dot_general(
                tok[:, cols], cot[...], FROM_LEFT, preferred_element_type=F32
            ).astype(BF16)
            for p in range(8):
                parts[p, xs, zz, 0] = part[:128, p * WIDTH : p * WIDTH + WIDTH]
                parts[p, xs, zz, 1] = part[128:, p * WIDTH : p * WIDTH + WIDTH]
            return carry

        lax.fori_loop(0, 4, block, 0)
        y1.append([send(parts.at[p, xs, :, oy], got_y.at[p, xs], y_peer) for p in Y_PIECES])
        if k == 0:
            for copy in gx + gz:
                copy.wait_recv()
            hx, hz = [None] * 3, [None] * 3
            for i in (1, 2, 0):
                hx[i] = same(wf.at[:, z, ylo, rows_x], z_peer[i])
                hz[i] = same(wf.at[x, :, ylo, rows_z], x_peer[i])
            for i in (1, 2, 0):
                far.append((same(wf.at[xk[i], z, ylo, rows_x], y_far, "far"), wf.at[xk[i], z, oy, rows_x]))
                far.append((same(wf.at[x, zk[i], ylo, rows_z], y_far, "far"), wf.at[x, zk[i], oy, rows_z]))

    def block_of(p, place, h):
        if p in X_PIECES:
            return parts.at[p, place, pl.ds(2 * h, 2)]
        return parts.at[p, pl.ds(2 * h, 2), place]

    def line(p):
        return (x, xk, x_peer) if p in X_PIECES else (z, zk, z_peer)

    s1 = {}

    def start_s1(p):
        _, places, peers = line(p)
        far_place, right, left = places[0], places[1], places[2]
        to_right, to_left = peers[1], peers[2]
        s1[p] = [
            send(block_of(p, far_place, 0), got_s1.at[p - 2, 0], to_right),
            send(block_of(p, far_place, 1), got_s1.at[p - 2, 1], to_left),
            send(block_of(p, right, 1), got_s1.at[p - 2, 2], to_right),
            send(block_of(p, left, 0), got_s1.at[p - 2, 3], to_left),
        ]

    def add_into(ref, sources, count):
        def one(i, carry):
            total = ref(i)[...].astype(F32)
            for source in sources:
                total += source(i)[...].astype(F32)
            ref(i)[...] = total.astype(BF16)
            return carry

        lax.fori_loop(0, count, one, 0)

    def chunk_of(p, place, h):
        if p in X_PIECES:
            return lambda c: parts.at[p, place, 2 * h + c // 2, c % 2]
        return lambda c: parts.at[p, 2 * h + c // 2, place, c % 2]

    def got(p, slot):
        return lambda c: got_s1.at[p - 2, slot, c // 2, c % 2]

    def pass_on(p):
        _, places, peers = line(p)
        right, left = places[1], places[2]
        s1[p][0].wait_recv()
        add_into(chunk_of(p, right, 0), [got(p, 0)], 4)
        s1[p].append(send(block_of(p, right, 0), got_s1.at[p - 2, 4], peers[1]))
        s1[p][1].wait_recv()
        add_into(chunk_of(p, left, 1), [got(p, 1)], 4)
        s1[p].append(send(block_of(p, left, 1), got_s1.at[p - 2, 5], peers[2]))

    def mine(p, c, y):
        if p in X_PIECES or p == Y_PIECES[0]:
            return parts.at[p, x, c, y]
        return parts.at[p, c, z, y]

    y2, last = {}, {}

    def finish_s1(p):
        place, _, _ = line(p)
        for copy in s1[p][2:]:
            copy.wait_recv()
        add_into(chunk_of(p, place, 0), [got(p, 3), got(p, 4)], 4)
        add_into(chunk_of(p, place, 1), [got(p, 2), got(p, 5)], 4)
        if p in X_PIECES:
            view = parts.at[p, x, :, oy]
        else:
            view = parts.at[p, :, z, oy]
        y2[p] = send(view, got_y2.at[p - 2], y_peer)

    def finish_y(p):
        y2[p].wait_recv()
        add_into(lambda c: mine(p, c, ylo), [lambda c: got_y2.at[p - 2, c]], 4)
        start_last(p)

    def start_last(p):
        peers, places = (z_peer, zk) if p in X_PIECES or p == Y_PIECES[0] else (x_peer, xk)
        last[p] = [send(mine(p, places[k], ylo), got_last.at[p, k], peers[k]) for k in range(3)]

    def input_grad(plane, base):
        def one(i, carry):
            xx, zz = i // 2, (i % 2) * 2
            rows = jnp.concatenate([wf[xx, zz, plane], wf[xx, zz + 1, plane]], axis=0)
            out = lax.dot_general(cot[...], rows, TURNED, preferred_element_type=F32).astype(BF16)
            ig[base + i, 0] = out[:, :128]
            ig[base + i, 1] = out[:, 128:]
            for j in range(2):
                cols = pl.ds(pl.multiple_of(((xx * 4 + zz + j) * 2 + plane) * 128, 128), 128)
                pltpu.make_async_copy(ig.at[base + i, j], ig_hbm.at[:, cols], ig_sem.at[base + i, j]).start()
            return carry

        lax.fori_loop(0, 8, one, 0)

    for p in (2, 5, 3, 6):
        start_s1(p)

    for i in (1, 2, 0):
        zs, xs = zk[(0, 2, 1)[i]], xk[(0, 2, 1)[i]]
        hx[i].wait_recv()
        far.append((same(wf.at[:, zs, ylo, rows_x], y_far, "far"), wf.at[:, zs, oy, rows_x]))
        hz[i].wait_recv()
        far.append((same(wf.at[xs, :, ylo, rows_z], y_far, "far"), wf.at[xs, :, oy, rows_z]))
    near = same(wf.at[:, :, ylo, rows_c], core_peer, "near")

    pass_on(2)
    pass_on(5)
    start_s1(4)
    start_s1(7)
    near.wait_recv()
    input_grad(ylo, 0)
    pass_on(3)
    pass_on(6)

    for k in range(4):
        xs = xk[k]
        for p in Y_PIECES:
            y1[k][p].wait_recv()
            add_into(
                lambda c, p=p, xs=xs: parts.at[p, xs, c, ylo], [lambda c, p=p, xs=xs: got_y.at[p, xs, c]], 4
            )
    x2 = [send(parts.at[0, xk[k], :, ylo], got_x2.at[k], x_peer[k]) for k in range(3)]
    z2 = [send(parts.at[1, :, zk[k], ylo], got_z2.at[k], z_peer[k]) for k in range(3)]
    pass_on(4)
    pass_on(7)
    finish_s1(2)
    finish_s1(5)

    def forward(count):
        for copy, view in far[:count]:
            copy.wait_recv()
            near2.append(same(view, core_peer, "far"))
        del far[:count]

    near2 = []
    forward(7)
    finish_s1(3)
    finish_s1(6)
    for copy in x2:
        copy.wait_recv()
    add_into(lambda c: mine(0, c, ylo), [lambda c, k=k: got_x2.at[k, c] for k in range(3)], 4)
    start_last(0)
    for copy in z2:
        copy.wait_recv()
    add_into(lambda c: mine(1, c, ylo), [lambda c, k=k: got_z2.at[k, c] for k in range(3)], 4)
    start_last(1)
    finish_y(2)
    finish_y(5)
    finish_s1(4)
    finish_s1(7)
    finish_y(3)
    finish_y(6)
    finish_y(4)
    finish_y(7)
    forward(6)

    mom_load.wait()
    for load in small:
        load.wait()
    for p in (0, 1, 2, 5, 3, 6, 4, 7):
        for copy in last[p]:
            copy.wait_recv()
        total = parts[p, x, z, ylo].astype(F32)
        for k in range(3):
            total += got_last[p, k].astype(F32)
        lo = p * WIDTH
        cur[:, lo : lo + WIDTH] = DECAY * mom[:, lo : lo + WIDTH] + total * (1.0 / np.sqrt(24576.0))
    rows, lanes = (rows_ref[0], rows_ref[1]), (lanes_ref[0], lanes_ref[1])
    coefs = to_coefs(cur[...], rows, lanes).reshape(2, 8, 8, 1024)
    me = lax.axis_index("rep")
    masks = kept_masks([kept_ref[me, a] for a in range(2)], tile_ref[...])
    folded, dense = [], []
    for which in range(2):
        for a in range(2):
            folded.append(jnp.sum(jnp.where(masks[which][a], coefs[a], 0.0), axis=0))
    ex[me] = dot_exact(jnp.concatenate(folded, axis=0), fold_ref[...])
    shared = [same(ex.at[me], peer, "ex") for peer in rep_peers]
    for a in range(2):
        dense.append(jnp.where(masks[0][a] | masks[1][a], coefs[a], 0.0).reshape(64, 1024))
    newmom[...] = cur[...] - from_coefs(jnp.concatenate(dense, axis=0), rows, lanes)
    newmom_store = pltpu.make_async_copy(newmom, newmom_hbm.at[0], local_sem.at[12])
    newmom_store.start()

    for copy in near2:
        copy.wait_recv()
    input_grad(oy, 8)
    for copy in shared:
        copy.wait_recv()
    ex_store = pltpu.make_async_copy(ex, ex_hbm, local_sem.at[13])
    ex_store.start()
    for copy in sent:
        copy.wait_send()

    def drain(i, carry):
        for j in range(2):
            pltpu.make_async_copy(ig.at[i, j], ig_hbm.at[:, pl.ds(0, 128)], ig_sem.at[i, j]).wait()
        return carry

    lax.fori_loop(0, 16, drain, 0)
    newmom_store.wait()
    ex_store.wait()


def last_kernel(
    ig_in, mom_in, ex_hbm, kept_hbm, w_hbm, rows_hbm, lanes_hbm, fold_hbm, tile_hbm, ones_hbm,
    ig_out, mom_out, neww_out, upd_out,
    ig, mom, ex_ref, w_ref, kept_ref, rows_ref, lanes_ref, fold_ref, tile_ref, ones_ref,
    neww_ref, upd_ref, sem,
):
    small = [
        (ex_hbm, ex_ref), (kept_hbm, kept_ref), (fold_hbm, fold_ref), (tile_hbm, tile_ref), (rows_hbm, rows_ref),
        (lanes_hbm, lanes_ref), (ones_hbm, ones_ref), (w_hbm, w_ref),
    ]
    small = [pltpu.make_async_copy(src, dst, sem.at[2, i]) for i, (src, dst) in enumerate(small)]
    for load in small:
        load.start()
    pieces = [(ig_in.at[pl.ds(i * 96, 96)], ig.at[pl.ds(i * 96, 96)], ig_out.at[pl.ds(i * 96, 96)]) for i in range(8)]
    pieces.append((mom_in, mom, mom_out))
    loads = [pltpu.make_async_copy(src, mid, sem.at[0, i]) for i, (src, mid, _) in enumerate(pieces)]
    stores = [pltpu.make_async_copy(mid, dst, sem.at[1, i]) for i, (_, mid, dst) in enumerate(pieces)]
    for load in loads:
        load.start()
    for load in small:
        load.wait()
    rows, lanes = (rows_ref[0], rows_ref[1]), (lanes_ref[0], lanes_ref[1])
    total = [jnp.zeros((8, 8, 1024), F32)] * 2
    wide = dot_exact(ex_ref[...].reshape(128, 128), fold_ref[...], TURNED).reshape(4, 2, 2, 8, 1024)
    for r in range(4):
        masks = kept_masks([kept_ref[r, a] for a in range(2)], tile_ref[...])
        for a in range(2):
            first = jnp.broadcast_to(wide[r, 0, a][None], (8, 8, 1024))
            second = jnp.broadcast_to(wide[r, 1, a][None], (8, 8, 1024))
            total[a] += jnp.where(masks[0][a], first, jnp.where(masks[1][a], second, 0.0))
    field = jnp.concatenate([t.reshape(64, 1024) for t in total], axis=0)
    for load, store in zip(loads, stores):
        load.wait()
        store.start()
    average = from_coefs(field, rows, lanes) * 0.25
    squares = jnp.sum((average * average).reshape(2, 64, 1024), axis=1)
    stacked = jnp.concatenate([squares[:, i * 128 : (i + 1) * 128] for i in range(8)], axis=0)
    means = dot_exact(stacked, ones_ref[...]) * (1.0 / (TILE * TILE))
    spread = jnp.sqrt(means + 1e-06)
    for i in range(8):
        for a in range(2):
            rows_a, cols = slice(a * 64, a * 64 + 64), slice(i * 128, i * 128 + 128)
            avg = average[rows_a, cols]
            update = avg / (jnp.abs(avg) + spread[i * 2 + a : i * 2 + a + 1])
            upd_ref[rows_a, cols] = update
            neww_ref[rows_a, cols] = w_ref[rows_a, cols] - STEP * update
    results = [(neww_ref, neww_out), (upd_ref, upd_out)]
    results = [pltpu.make_async_copy(src, dst, sem.at[1, 9 + i]) for i, (src, dst) in enumerate(results)]
    for store in results:
        store.start()
    for store in stores + results:
        store.wait()


def body(tokens, cotangent, weight, momentum, kept):
    any_space = pl.BlockSpec(memory_space=pl.ANY)
    rows, lanes = jnp.asarray(two_halves(dct_matrix(2))), jnp.asarray(two_halves(dct_matrix(4)))
    fold, tile_lane = jnp.asarray(fold_matrix()), jnp.asarray(tile_lanes())
    ones = jnp.asarray(np.kron(np.eye(2), np.ones((TILE, TILE))).astype(jnp.bfloat16))
    kept = kept.transpose(0, 1, 3, 2)
    constants = [
        pltpu.VMEM((4, 2, 2, 16), jnp.int32),
        pltpu.VMEM((2, 128, 128), BF16),
        pltpu.VMEM((2, 256, 256), BF16),
        pltpu.VMEM((1024, 128), BF16),
        pltpu.VMEM((16, 1024), BF16),
    ]
    sems = 160
    ig, newmom, shared = pl.pallas_call(
        main_kernel,
        out_shape=(
            jax.ShapeDtypeStruct((768, 4096), BF16),
            jax.ShapeDtypeStruct((1, 128, 1024), F32),
            jax.ShapeDtypeStruct((4, 32, 128), F32),
        ),
        in_specs=[any_space] * 9,
        out_specs=(any_space, any_space, any_space),
        scratch_shapes=[
            pltpu.VMEM((768, 4096), BF16),
            pltpu.VMEM((768, 1024), BF16),
            pltpu.VMEM((128, 1024), F32),
            pltpu.VMEM((128, 1024), F32),
            *constants,
            pltpu.VMEM((4, 4, 2, 128, 1024), BF16),
            pltpu.VMEM((8, 4, 4, 2, 128, WIDTH), BF16),
            pltpu.VMEM((2, 4, 4, 128, WIDTH), BF16),
            pltpu.VMEM((6, 6, 2, 2, 128, WIDTH), BF16),
            pltpu.VMEM((3, 4, 128, WIDTH), BF16),
            pltpu.VMEM((3, 4, 128, WIDTH), BF16),
            pltpu.VMEM((6, 4, 128, WIDTH), BF16),
            pltpu.VMEM((8, 3, 128, WIDTH), BF16),
            pltpu.VMEM((16, 2, 768, 128), BF16),
            pltpu.VMEM((128, 1024), F32),
            pltpu.VMEM((128, 1024), F32),
            pltpu.VMEM((4, 32, 128), F32),
            pltpu.SemaphoreType.DMA((14,)),
            pltpu.SemaphoreType.DMA((16, 2)),
            pltpu.SemaphoreType.DMA((sems,)),
            pltpu.SemaphoreType.DMA((sems,)),
        ],
        compiler_params=pltpu.CompilerParams(
            collective_id=0, has_side_effects=True, vmem_limit_bytes=60 << 20
        ),
        cost_estimate=pl.CostEstimate(flops=13 * 10**9, bytes_accessed=20 * 10**6, transcendentals=0),
        name="gradients",
    )(tokens, cotangent, weight, momentum, kept, rows, lanes, fold, tile_lane)
    return pl.pallas_call(
        last_kernel,
        out_shape=(
            jax.ShapeDtypeStruct((768, 4096), BF16),
            jax.ShapeDtypeStruct((1, 128, 1024), F32),
            jax.ShapeDtypeStruct((128, 1024), F32),
            jax.ShapeDtypeStruct((128, 1024), F32),
        ),
        in_specs=[any_space] * 10,
        out_specs=(any_space, any_space, any_space, any_space),
        scratch_shapes=[
            pltpu.VMEM((768, 4096), BF16),
            pltpu.VMEM((1, 128, 1024), F32),
            pltpu.VMEM((4, 32, 128), F32),
            pltpu.VMEM((128, 1024), F32),
            *constants,
            pltpu.VMEM((128, 128), BF16),
            pltpu.VMEM((128, 1024), F32),
            pltpu.VMEM((128, 1024), F32),
            pltpu.SemaphoreType.DMA((3, 12)),
        ],
        compiler_params=pltpu.CompilerParams(vmem_limit_bytes=60 << 20),
        name="step",
    )(ig, newmom, shared, kept, weight, rows, lanes, fold, tile_lane, ones)


def solution(mesh):
    in_specs = (
        P(("rep", "fsdp"), None),
        P(("rep", "fsdp"), None),
        P("fsdp", None),
        P("rep", "fsdp", None),
        P(None, "fsdp", None, None),
    )
    out_specs = (P(("rep", "fsdp"), None), P("rep", "fsdp", None), P("fsdp", None), P("fsdp", None))
    return jax.shard_map(body, mesh=mesh, in_specs=in_specs, out_specs=out_specs, check_vma=False)
```

```python
import jax
import jax.numpy as jnp
import numpy as np
from jax import lax
from jax.experimental import pallas as pl
from jax.experimental.pallas import tpu as pltpu
from jax.sharding import PartitionSpec as P

TILE = 64
BLK = 8
DECAY = 0.999
STEP = 0.02
MESH = pl.DeviceIdType.MESH
F32 = jnp.float32
BF16 = jnp.bfloat16

WIDTH = 128
Y_PIECES, X_PIECES, Z_PIECES = (0, 1), (2, 3, 4), (5, 6, 7)
OFFS = (2, 1, 3, 0)


def dct_matrix(copies):
    freq = np.arange(TILE, dtype=np.float64)[:, None]
    place = np.arange(TILE, dtype=np.float64)[None, :]
    table = np.cos(np.pi * (2.0 * place + 1.0) * freq / (2.0 * TILE))
    table *= np.where(freq == 0.0, np.sqrt(1.0 / TILE), np.sqrt(2.0 / TILE))
    return np.kron(np.eye(copies), table).astype(np.float32)


def two_halves(matrix):
    high = matrix.astype(jnp.bfloat16)
    low = (matrix - high.astype(np.float32)).astype(jnp.bfloat16)
    return np.stack([high, low])


def fold_matrix():
    fold = np.zeros((1024, 128), np.float32)
    lane = np.arange(1024)
    fold[lane, (lane // TILE) * BLK + lane % BLK] = 1.0
    return fold.astype(jnp.bfloat16)


PLAIN = (((1,), (0,)), ((), ()))
TURNED = (((1,), (1,)), ((), ()))
FROM_LEFT = (((0,), (0,)), ((), ()))


def dot(a, b, dims=PLAIN):
    return lax.dot_general(a, b, dims, preferred_element_type=F32)


def halves(a):
    high = a.astype(BF16)
    return high, (a - high.astype(F32)).astype(BF16)


def dot_marks(a, marks, dims=PLAIN):
    count = a.shape[0]
    high = a.astype(BF16)
    rest = a - high.astype(F32)
    mid = rest.astype(BF16)
    low = (rest - mid.astype(F32)).astype(BF16)
    out = dot(jnp.concatenate([high, mid, low], axis=0), marks, dims)
    return out[:count] + (out[count : 2 * count] + out[2 * count :])


def dot_left(table, field, dims=PLAIN):
    high, low = halves(field)
    if dims is FROM_LEFT:
        return dot(table[0], high, dims) + (dot(table[0], low, dims) + dot(table[1], high, dims))
    count = table.shape[1]
    out = dot(table.reshape(2 * count, count), high, dims)
    return out[:count] + (out[count:] + dot(table[0], low, dims))


def dot_right(field, table, dims=PLAIN):
    count = field.shape[0]
    high, low = halves(field)
    out = dot(jnp.concatenate([high, low], axis=0), table[0], dims)
    return out[:count] + (out[count:] + dot(high, table[1], dims))


def side_by_side(field, width):
    return jnp.concatenate([field[:, i : i + width] for i in range(0, 1024, width)], axis=0)


def from_coefs(coefs, rows):
    count = coefs.shape[0]
    none = jnp.zeros((128, 128), BF16)
    lanes = [
        jnp.concatenate([jnp.concatenate([r, none], axis=1), jnp.concatenate([none, r], axis=1)], axis=0)
        for r in (rows[0], rows[1])
    ]
    mid = side_by_side(dot_left(rows, coefs, FROM_LEFT), 256)
    out = dot_right(mid, lanes)
    return jnp.concatenate([out[i * count : i * count + count] for i in range(4)], axis=1)


def block_numbers(width):
    number = lax.broadcasted_iota(jnp.int32, (8, 8, width), 0) * 8 + (
        lax.broadcasted_iota(jnp.int32, (8, 8, width), 2) % TILE
    ) // BLK
    return number.astype(F32)


def kept_lanes(kept):
    tile = lax.broadcasted_iota(jnp.int32, (16, 1024), 0)
    marks = jnp.where(tile == lax.broadcasted_iota(jnp.int32, (16, 1024), 1) // TILE, 1.0, 0.0)
    return dot(kept.astype(F32).astype(BF16), marks.astype(BF16))


def make_places():
    rep, shard = lax.axis_index("rep"), lax.axis_index("fsdp")
    yhi, core = rep // 2, rep % 2
    x, z, ylo = shard // 8, (shard // 2) % 4, shard % 2

    def at(yhi_=None, core_=None, x_=None, z_=None, ylo_=None):
        h = yhi if yhi_ is None else yhi_
        c = core if core_ is None else core_
        xx = x if x_ is None else x_
        zz = z if z_ is None else z_
        l = ylo if ylo_ is None else ylo_
        return (h * 2 + c, (xx * 4 + zz) * 2 + l)

    return yhi, core, x, z, ylo, at


def main_kernel(
    tok_hbm, cot_hbm, w_hbm, mom_hbm, kept_hbm, rows_hbm, fold_hbm,
    ig_hbm, newmom_hbm, ex_hbm,
    tok, cot, w, mom, kept_ref, rows_ref, fold_ref,
    wf, parts, got_y, got_s1, got_x2, got_z2, got_y2, got_last,
    ig, cur, newmom, dense, numbers, ex, local_sem, ig_sem, send_sem, recv_sem,
):
    yhi, core, x, z, ylo, at = make_places()
    oy = 1 - ylo
    xk = [lax.rem(x + o, 4) for o in OFFS]
    zk = [lax.rem(z + o, 4) for o in OFFS]
    x_peer = [at(x_=xk[k]) for k in range(3)]
    z_peer = [at(z_=zk[k]) for k in range(3)]
    y_peer = at(ylo_=oy)
    y_far = at(yhi_=1 - yhi, ylo_=oy)
    core_peer = at(core_=1 - core)
    rep_peers = [at(yhi_=1 - yhi), at(yhi_=1 - yhi, core_=1 - core), core_peer]

    half = pl.multiple_of(core * 64, 64)
    w_load = pltpu.make_async_copy(w_hbm.at[pl.ds(half, 64)], w, local_sem.at[0])
    cot_load = pltpu.make_async_copy(cot_hbm, cot, local_sem.at[1])
    mom_load = pltpu.make_async_copy(mom_hbm.at[0], mom, local_sem.at[2])
    tok_loads = []
    for k in range(4):
        cols = pl.ds(pl.multiple_of(xk[k] * 1024, 1024), 1024)
        tok_loads.append(pltpu.make_async_copy(tok_hbm.at[:, cols], tok.at[:, cols], local_sem.at[3 + k]))
    w_load.start()
    cot_load.start()
    for load in tok_loads:
        load.start()
    mom_load.start()
    small = [(kept_hbm, kept_ref), (rows_hbm, rows_ref), (fold_hbm, fold_ref)]
    small = [pltpu.make_async_copy(src, dst, local_sem.at[7 + i]) for i, (src, dst) in enumerate(small)]
    for load in small:
        load.start()

    barrier = pltpu.get_barrier_semaphore()
    everyone = x_peer + z_peer + [y_peer, y_far] + rep_peers
    for peer in everyone:
        pl.semaphore_signal(barrier, inc=1, device_id=peer, device_id_type=MESH)

    used = [0]
    sent = []

    def send(src, dst, peer, tag="rs"):
        n = used[0]
        used[0] += 1
        copy = pltpu.make_async_remote_copy(
            src_ref=src, dst_ref=dst, send_sem=send_sem.at[n], recv_sem=recv_sem.at[n],
            device_id=peer, device_id_type=MESH,
        )
        copy.start()
        sent.append(copy)
        return copy

    def same(view, peer, tag="ag"):
        return send(view, view, peer, tag)

    w_load.wait()
    rows_x, rows_z = pl.ds(half, 32), pl.ds(pl.multiple_of(half + 32, 32), 32)
    rows_c = pl.ds(half, 64)
    wf[x, z, ylo, rows_c] = w[...].astype(BF16)
    pl.semaphore_wait(barrier, len(everyone))
    gx = [same(wf.at[x, z, ylo, rows_x], peer) for peer in x_peer]
    gz = [same(wf.at[x, z, ylo, rows_z], peer) for peer in z_peer]
    far = [(same(wf.at[x, z, ylo, rows_c], y_far, "far"), wf.at[x, z, oy, rows_c])]

    cot_load.wait()
    y1 = []
    for k in range(4):
        xs = xk[k]
        tok_loads[k].wait()

        def block(zz, carry, xs=xs):
            cols = pl.ds(pl.multiple_of((xs * 4 + zz) * 256, 256), 256)
            part = lax.dot_general(
                tok[:, cols], cot[...], FROM_LEFT, preferred_element_type=F32
            ).astype(BF16)
            for p in range(8):
                parts[p, xs, zz, 0] = part[:128, p * WIDTH : p * WIDTH + WIDTH]
                parts[p, xs, zz, 1] = part[128:, p * WIDTH : p * WIDTH + WIDTH]
            return carry

        lax.fori_loop(0, 4, block, 0)
        y1.append([send(parts.at[p, xs, :, oy], got_y.at[p, xs], y_peer) for p in Y_PIECES])
        if k == 0:
            for copy in gx + gz:
                copy.wait_recv()
            hx, hz = [None] * 3, [None] * 3
            for i in (1, 2):
                hx[i] = same(wf.at[:, z, ylo, rows_x], z_peer[i])
                hz[i] = same(wf.at[x, :, ylo, rows_z], x_peer[i])
            for i in (1, 2, 0):
                far.append((same(wf.at[xk[i], z, ylo, rows_x], y_far, "far"), wf.at[xk[i], z, oy, rows_x]))
                far.append((same(wf.at[x, zk[i], ylo, rows_z], y_far, "far"), wf.at[x, zk[i], oy, rows_z]))

    def block_of(p, place, h):
        if p in X_PIECES:
            return parts.at[p, place, pl.ds(2 * h, 2)]
        return parts.at[p, pl.ds(2 * h, 2), place]

    def line(p):
        return (x, xk, x_peer) if p in X_PIECES else (z, zk, z_peer)

    s1 = {}

    def start_s1(p):
        _, places, peers = line(p)
        far_place, right, left = places[0], places[1], places[2]
        to_right, to_left = peers[1], peers[2]
        s1[p] = [
            send(block_of(p, far_place, 0), got_s1.at[p - 2, 0], to_right),
            send(block_of(p, far_place, 1), got_s1.at[p - 2, 1], to_left),
            send(block_of(p, right, 1), got_s1.at[p - 2, 2], to_right),
            send(block_of(p, left, 0), got_s1.at[p - 2, 3], to_left),
        ]

    def add_into(ref, sources, count):
        def one(i, carry):
            total = ref(i)[...].astype(F32)
            for source in sources:
                total += source(i)[...].astype(F32)
            ref(i)[...] = total.astype(BF16)
            return carry

        lax.fori_loop(0, count, one, 0)

    def chunk_of(p, place, h):
        if p in X_PIECES:
            return lambda c: parts.at[p, place, 2 * h + c // 2, c % 2]
        return lambda c: parts.at[p, 2 * h + c // 2, place, c % 2]

    def got(p, slot):
        return lambda c: got_s1.at[p - 2, slot, c // 2, c % 2]

    def pass_on(p):
        _, places, peers = line(p)
        right, left = places[1], places[2]
        s1[p][0].wait_recv()
        add_into(chunk_of(p, right, 0), [got(p, 0)], 4)
        s1[p].append(send(block_of(p, right, 0), got_s1.at[p - 2, 4], peers[1]))
        s1[p][1].wait_recv()
        add_into(chunk_of(p, left, 1), [got(p, 1)], 4)
        s1[p].append(send(block_of(p, left, 1), got_s1.at[p - 2, 5], peers[2]))

    def mine(p, c, y):
        if p in X_PIECES or p == Y_PIECES[0]:
            return parts.at[p, x, c, y]
        return parts.at[p, c, z, y]

    y2, last = {}, {}

    def finish_s1(p):
        place, _, _ = line(p)
        for copy in s1[p][2:]:
            copy.wait_recv()
        add_into(chunk_of(p, place, 0), [got(p, 3), got(p, 4)], 4)
        add_into(chunk_of(p, place, 1), [got(p, 2), got(p, 5)], 4)
        if p in X_PIECES:
            view = parts.at[p, x, :, oy]
        else:
            view = parts.at[p, :, z, oy]
        y2[p] = send(view, got_y2.at[p - 2], y_peer)

    def finish_y(p):
        y2[p].wait_recv()
        add_into(lambda c: mine(p, c, ylo), [lambda c: got_y2.at[p - 2, c]], 4)
        start_last(p)

    def start_last(p):
        peers, places = (z_peer, zk) if p in X_PIECES or p == Y_PIECES[0] else (x_peer, xk)
        last[p] = [send(mine(p, places[k], ylo), got_last.at[p, k], peers[k]) for k in range(3)]

    me = lax.axis_index("rep")

    def prepare():
        mom_load.wait()
        for load in small:
            load.wait()
        numbers[...] = kept_lanes(kept_ref[me])
        ex[me] = jnp.zeros((32, 128), F32)

    def finish(p):
        for copy in last[p]:
            copy.wait_recv()
        total = parts[p, x, z, ylo].astype(F32)
        for k in range(3):
            total += got_last[p, k].astype(F32)
        cols = slice(p * WIDTH, p * WIDTH + WIDTH)
        current = DECAY * mom[:, cols] + total * (1.0 / np.sqrt(24576.0))
        cur[:, cols] = current
        mid = dot_left(rows_ref[...], current)
        coefs = dot_right(mid, rows_ref[...], TURNED).reshape(2, 8, 8, WIDTH)
        places = block_numbers(WIDTH)
        masks = [
            [
                places == jnp.broadcast_to(numbers[2 * a + which, cols].reshape(1, 1, WIDTH), (8, 8, WIDTH))
                for a in range(2)
            ]
            for which in range(2)
        ]
        folded = [
            jnp.sum(jnp.where(masks[which][a], coefs[a], 0.0), axis=0) for which in range(2) for a in range(2)
        ]
        ex[me] += dot_marks(jnp.concatenate(folded, axis=0), fold_ref[cols])
        for a in range(2):
            kept_here = jnp.where(masks[0][a] | masks[1][a], coefs[a], 0.0)
            dense[a * 64 : a * 64 + 64, cols] = kept_here.reshape(64, WIDTH)

    def input_grad(plane, base, low, high):
        def one(i, carry):
            xx, zz = i // 2, (i % 2) * 2
            rows = jnp.concatenate([wf[xx, zz, plane], wf[xx, zz + 1, plane]], axis=0)
            out = lax.dot_general(cot[...], rows, TURNED, preferred_element_type=F32).astype(BF16)
            ig[base + i, 0] = out[:, :128]
            ig[base + i, 1] = out[:, 128:]
            for j in range(2):
                cols = pl.ds(pl.multiple_of(((xx * 4 + zz + j) * 2 + plane) * 128, 128), 128)
                pltpu.make_async_copy(ig.at[base + i, j], ig_hbm.at[:, cols], ig_sem.at[base + i, j]).start()
            return carry

        lax.fori_loop(low, high, one, 0)

    onward = []
    for i in (1, 2):
        zs, xs = zk[3 - i], xk[3 - i]
        pair = pl.ds(2 * (i - 1), 2)
        hx[i].wait_recv()
        onward.append(same(wf.at[pair, zs, ylo, rows_x], z_peer[i]))
        far.append((same(wf.at[:, zs, ylo, rows_x], y_far, "far"), wf.at[:, zs, oy, rows_x]))
        hz[i].wait_recv()
        onward.append(same(wf.at[xs, pair, ylo, rows_z], x_peer[i]))
        far.append((same(wf.at[xs, :, ylo, rows_z], y_far, "far"), wf.at[xs, :, oy, rows_z]))
    for p in (2, 5, 3, 6):
        start_s1(p)
    pass_on(2)
    pass_on(5)
    start_s1(4)
    start_s1(7)
    for copy in onward:
        copy.wait_recv()
    far.append((same(wf.at[:, zk[0], ylo, rows_x], y_far, "far"), wf.at[:, zk[0], oy, rows_x]))
    far.append((same(wf.at[xk[0], :, ylo, rows_z], y_peer, "far"), wf.at[xk[0], :, oy, rows_z]))
    near = same(wf.at[:, :, ylo, rows_c], core_peer, "near")
    near.wait_recv()
    input_grad(ylo, 0, 0, 8)
    pass_on(3)
    pass_on(6)

    prepare()
    for k in range(4):
        xs = xk[k]
        for p in Y_PIECES:
            y1[k][p].wait_recv()
            add_into(
                lambda c, p=p, xs=xs: parts.at[p, xs, c, ylo], [lambda c, p=p, xs=xs: got_y.at[p, xs, c]], 4
            )
    pass_on(4)
    pass_on(7)
    x2 = [send(parts.at[0, xk[k], :, ylo], got_x2.at[k], x_peer[k]) for k in range(3)]
    z2 = [send(parts.at[1, :, zk[k], ylo], got_z2.at[k], z_peer[k]) for k in range(3)]
    finish_s1(2)
    finish_s1(5)

    def forward(count):
        for copy, view in far[:count]:
            copy.wait_recv()
            near2.append(same(view, core_peer, "far"))
        del far[:count]

    near2 = []
    forward(7)
    finish_s1(3)
    finish_s1(6)
    finish_y(2)
    finish_y(5)
    finish_s1(4)
    finish_s1(7)
    for copy in x2:
        copy.wait_recv()
    add_into(lambda c: mine(0, c, ylo), [lambda c, k=k: got_x2.at[k, c] for k in range(3)], 4)
    start_last(0)
    for copy in z2:
        copy.wait_recv()
    add_into(lambda c: mine(1, c, ylo), [lambda c, k=k: got_z2.at[k, c] for k in range(3)], 4)
    start_last(1)
    finish_y(3)
    finish_y(6)
    forward(6)
    finish(2)
    finish(5)
    finish_y(4)
    finish_y(7)
    for copy in near2:
        copy.wait_recv()
    input_grad(oy, 8, 0, 4)
    finish(3)
    finish(6)
    finish(0)
    finish(1)
    finish(4)
    finish(7)
    shared = [same(ex.at[me], peer, "ex") for peer in rep_peers]
    newmom[...] = cur[...] - from_coefs(dense[...], rows_ref[...])
    newmom_store = pltpu.make_async_copy(newmom, newmom_hbm.at[0], local_sem.at[12])
    newmom_store.start()

    input_grad(oy, 8, 4, 8)
    for copy in shared:
        copy.wait_recv()
    ex_store = pltpu.make_async_copy(ex, ex_hbm, local_sem.at[13])
    ex_store.start()
    for copy in sent:
        copy.wait_send()

    def drain(i, carry):
        for j in range(2):
            pltpu.make_async_copy(ig.at[i, j], ig_hbm.at[:, pl.ds(0, 128)], ig_sem.at[i, j]).wait()
        return carry

    lax.fori_loop(0, 16, drain, 0)
    newmom_store.wait()
    ex_store.wait()


def last_kernel(
    ig_in, mom_in, ex_hbm, kept_hbm, w_hbm, rows_hbm, fold_hbm, ones_hbm,
    ig_out, mom_out, neww_out, upd_out,
    ig, mom, ex_ref, w_ref, kept_ref, rows_ref, fold_ref, ones_ref,
    neww_ref, upd_ref, sem,
):
    small = [
        (ex_hbm, ex_ref), (kept_hbm, kept_ref), (fold_hbm, fold_ref), (rows_hbm, rows_ref), (ones_hbm, ones_ref),
        (w_hbm, w_ref),
    ]
    small = [pltpu.make_async_copy(src, dst, sem.at[2, i]) for i, (src, dst) in enumerate(small)]
    for load in small:
        load.start()
    pieces = [(ig_in.at[pl.ds(i * 96, 96)], ig.at[pl.ds(i * 96, 96)], ig_out.at[pl.ds(i * 96, 96)]) for i in range(8)]
    pieces.append((mom_in, mom, mom_out))
    loads = [pltpu.make_async_copy(src, mid, sem.at[0, i]) for i, (src, mid, _) in enumerate(pieces)]
    stores = [pltpu.make_async_copy(mid, dst, sem.at[1, i]) for i, (_, mid, dst) in enumerate(pieces)]
    for load in loads:
        load.start()
    for load in small:
        load.wait()
    total = [jnp.zeros((8, 8, 1024), F32)] * 2
    wide = dot_marks(ex_ref[...].reshape(128, 128), fold_ref[...], TURNED).reshape(4, 2, 2, 8, 1024)
    numbers = kept_lanes(kept_ref[...].reshape(16, 16))
    places = block_numbers(1024)
    for r in range(4):
        for a in range(2):
            value = 0.0
            for which in (1, 0):
                at = r * 4 + a * 2 + which
                mask = places == jnp.broadcast_to(numbers[at : at + 1].reshape(1, 1, 1024), (8, 8, 1024))
                value = jnp.where(mask, jnp.broadcast_to(wide[r, which, a][None], (8, 8, 1024)), value)
            total[a] += value
        for load, store in list(zip(loads, stores))[2 * r : 2 * r + 2 + r // 3]:
            load.wait()
            store.start()
    field = jnp.concatenate([t.reshape(64, 1024) for t in total], axis=0)
    average = from_coefs(field, rows_ref[...]) * 0.25
    squares = jnp.sum((average * average).reshape(2, 64, 1024), axis=1)
    means = dot_marks(side_by_side(squares, 128), ones_ref[...]) * (1.0 / (TILE * TILE))
    spread = jnp.sqrt(means + 1e-06)
    for i in range(8):
        for a in range(2):
            rows_a, cols = slice(a * 64, a * 64 + 64), slice(i * 128, i * 128 + 128)
            avg = average[rows_a, cols]
            update = avg / (jnp.abs(avg) + spread[i * 2 + a : i * 2 + a + 1])
            upd_ref[rows_a, cols] = update
            neww_ref[rows_a, cols] = w_ref[rows_a, cols] - STEP * update
    results = [(neww_ref, neww_out), (upd_ref, upd_out)]
    results = [pltpu.make_async_copy(src, dst, sem.at[1, 9 + i]) for i, (src, dst) in enumerate(results)]
    for store in results:
        store.start()
    for store in stores + results:
        store.wait()


def body(tokens, cotangent, weight, momentum, kept):
    any_space = pl.BlockSpec(memory_space=pl.ANY)
    rows, fold = jnp.asarray(two_halves(dct_matrix(2))), jnp.asarray(fold_matrix())
    ones = jnp.asarray(np.kron(np.eye(2), np.ones((TILE, TILE))).astype(jnp.bfloat16))
    kept = kept.transpose(0, 1, 3, 2).reshape(4, 4, 16)
    constants = [
        pltpu.VMEM((4, 4, 16), jnp.int32),
        pltpu.VMEM((2, 128, 128), BF16),
        pltpu.VMEM((1024, 128), BF16),
    ]
    sems = 160
    ig, newmom, shared = pl.pallas_call(
        main_kernel,
        out_shape=(
            jax.ShapeDtypeStruct((768, 4096), BF16),
            jax.ShapeDtypeStruct((1, 128, 1024), F32),
            jax.ShapeDtypeStruct((4, 32, 128), F32),
        ),
        in_specs=[any_space] * 7,
        out_specs=(any_space, any_space, any_space),
        scratch_shapes=[
            pltpu.VMEM((768, 4096), BF16),
            pltpu.VMEM((768, 1024), BF16),
            pltpu.VMEM((64, 1024), F32),
            pltpu.VMEM((128, 1024), F32),
            *constants,
            pltpu.VMEM((4, 4, 2, 128, 1024), BF16),
            pltpu.VMEM((8, 4, 4, 2, 128, WIDTH), BF16),
            pltpu.VMEM((2, 4, 4, 128, WIDTH), BF16),
            pltpu.VMEM((6, 6, 2, 2, 128, WIDTH), BF16),
            pltpu.VMEM((3, 4, 128, WIDTH), BF16),
            pltpu.VMEM((3, 4, 128, WIDTH), BF16),
            pltpu.VMEM((6, 4, 128, WIDTH), BF16),
            pltpu.VMEM((8, 3, 128, WIDTH), BF16),
            pltpu.VMEM((16, 2, 768, 128), BF16),
            pltpu.VMEM((128, 1024), F32),
            pltpu.VMEM((128, 1024), F32),
            pltpu.VMEM((128, 1024), F32),
            pltpu.VMEM((4, 1024), F32),
            pltpu.VMEM((4, 32, 128), F32),
            pltpu.SemaphoreType.DMA((14,)),
            pltpu.SemaphoreType.DMA((16, 2)),
            pltpu.SemaphoreType.DMA((sems,)),
            pltpu.SemaphoreType.DMA((sems,)),
        ],
        compiler_params=pltpu.CompilerParams(
            collective_id=0, has_side_effects=True, vmem_limit_bytes=60 << 20
        ),
        cost_estimate=pl.CostEstimate(flops=13 * 10**9, bytes_accessed=20 * 10**6, transcendentals=0),
        name="gradients",
    )(tokens, cotangent, weight, momentum, kept, rows, fold)
    return pl.pallas_call(
        last_kernel,
        out_shape=(
            jax.ShapeDtypeStruct((768, 4096), BF16),
            jax.ShapeDtypeStruct((1, 128, 1024), F32),
            jax.ShapeDtypeStruct((128, 1024), F32),
            jax.ShapeDtypeStruct((128, 1024), F32),
        ),
        in_specs=[any_space] * 8,
        out_specs=(any_space, any_space, any_space, any_space),
        scratch_shapes=[
            pltpu.VMEM((768, 4096), BF16),
            pltpu.VMEM((1, 128, 1024), F32),
            pltpu.VMEM((4, 32, 128), F32),
            pltpu.VMEM((128, 1024), F32),
            *constants,
            pltpu.VMEM((128, 128), BF16),
            pltpu.VMEM((128, 1024), F32),
            pltpu.VMEM((128, 1024), F32),
            pltpu.SemaphoreType.DMA((3, 12)),
        ],
        compiler_params=pltpu.CompilerParams(vmem_limit_bytes=60 << 20),
        name="step",
    )(ig, newmom, shared, kept, weight, rows, fold, ones)


def solution(mesh):
    in_specs = (
        P(("rep", "fsdp"), None),
        P(("rep", "fsdp"), None),
        P("fsdp", None),
        P("rep", "fsdp", None),
        P(None, "fsdp", None, None),
    )
    out_specs = (P(("rep", "fsdp"), None), P("rep", "fsdp", None), P("fsdp", None), P("fsdp", None))
    return jax.shard_map(body, mesh=mesh, in_specs=in_specs, out_specs=out_specs, check_vma=False)
```

```python
import jax
import jax.numpy as jnp
import numpy as np
from jax import lax
from jax.experimental import pallas as pl
from jax.experimental.pallas import tpu as pltpu
from jax.sharding import PartitionSpec as P

TILE = 64
BLK = 8
DECAY = 0.999
STEP = 0.02
MESH = pl.DeviceIdType.MESH
F32 = jnp.float32
BF16 = jnp.bfloat16

WIDTH = 128
Y_PIECES, X_PIECES, Z_PIECES = (0, 1), (2, 3, 4), (5, 6, 7)
OFFS = (2, 1, 3, 0)


def dct_matrix(copies):
    freq = np.arange(TILE, dtype=np.float64)[:, None]
    place = np.arange(TILE, dtype=np.float64)[None, :]
    table = np.cos(np.pi * (2.0 * place + 1.0) * freq / (2.0 * TILE))
    table *= np.where(freq == 0.0, np.sqrt(1.0 / TILE), np.sqrt(2.0 / TILE))
    return np.kron(np.eye(copies), table).astype(np.float32)


def two_halves(matrix):
    high = matrix.astype(jnp.bfloat16)
    low = (matrix - high.astype(np.float32)).astype(jnp.bfloat16)
    return np.stack([high, low])


def fold_matrix():
    fold = np.zeros((1024, 128), np.float32)
    lane = np.arange(1024)
    fold[lane, (lane // TILE) * BLK + lane % BLK] = 1.0
    return fold.astype(jnp.bfloat16)


PLAIN = (((1,), (0,)), ((), ()))
TURNED = (((1,), (1,)), ((), ()))
FROM_LEFT = (((0,), (0,)), ((), ()))


def dot(a, b, dims=PLAIN):
    return lax.dot_general(a, b, dims, preferred_element_type=F32)


def halves(a):
    high = a.astype(BF16)
    return high, (a - high.astype(F32)).astype(BF16)


def dot_marks(a, marks, dims=PLAIN):
    count = a.shape[0]
    high = a.astype(BF16)
    rest = a - high.astype(F32)
    mid = rest.astype(BF16)
    low = (rest - mid.astype(F32)).astype(BF16)
    out = dot(jnp.concatenate([high, mid, low], axis=0), marks, dims)
    return out[:count] + (out[count : 2 * count] + out[2 * count :])


def dot_left(table, field, dims=PLAIN):
    high, low = halves(field)
    if dims is FROM_LEFT:
        return dot(table[0], high, dims) + (dot(table[0], low, dims) + dot(table[1], high, dims))
    count = table.shape[1]
    out = dot(table.reshape(2 * count, count), high, dims)
    return out[:count] + (out[count:] + dot(table[0], low, dims))


def dot_right(field, table, dims=PLAIN):
    count = field.shape[0]
    high, low = halves(field)
    out = dot(jnp.concatenate([high, low], axis=0), table[0], dims)
    return out[:count] + (out[count:] + dot(high, table[1], dims))


def side_by_side(field, width):
    return jnp.concatenate([field[:, i : i + width] for i in range(0, 1024, width)], axis=0)


def from_coefs(coefs, rows):
    count = coefs.shape[0]
    none = jnp.zeros((128, 128), BF16)
    lanes = [
        jnp.concatenate([jnp.concatenate([r, none], axis=1), jnp.concatenate([none, r], axis=1)], axis=0)
        for r in (rows[0], rows[1])
    ]
    mid = side_by_side(dot_left(rows, coefs, FROM_LEFT), 256)
    out = dot_right(mid, lanes)
    return jnp.concatenate([out[i * count : i * count + count] for i in range(4)], axis=1)


def block_numbers(width):
    number = lax.broadcasted_iota(jnp.int32, (8, 8, width), 0) * 8 + (
        lax.broadcasted_iota(jnp.int32, (8, 8, width), 2) % TILE
    ) // BLK
    return number.astype(F32)


def kept_lanes(kept):
    tile = lax.broadcasted_iota(jnp.int32, (16, 1024), 0)
    marks = jnp.where(tile == lax.broadcasted_iota(jnp.int32, (16, 1024), 1) // TILE, 1.0, 0.0)
    return dot(kept.astype(F32).astype(BF16), marks.astype(BF16))


def make_places():
    rep, shard = lax.axis_index("rep"), lax.axis_index("fsdp")
    yhi, core = rep // 2, rep % 2
    x, z, ylo = shard // 8, (shard // 2) % 4, shard % 2

    def at(yhi_=None, core_=None, x_=None, z_=None, ylo_=None):
        h = yhi if yhi_ is None else yhi_
        c = core if core_ is None else core_
        xx = x if x_ is None else x_
        zz = z if z_ is None else z_
        l = ylo if ylo_ is None else ylo_
        return (h * 2 + c, (xx * 4 + zz) * 2 + l)

    return yhi, core, x, z, ylo, at


def main_kernel(
    tok_hbm, cot_hbm, w_hbm, mom_hbm, kept_hbm, rows_hbm, fold_hbm,
    ig, newmom, ex_out,
    tok, cot, w, mom, kept_ref, rows_ref, fold_ref,
    wf, parts, got_y, got_s1, got_x2, got_z2, got_y2, got_last,
    cur, dense, numbers, ex, local_sem, send_sem, recv_sem,
):
    yhi, core, x, z, ylo, at = make_places()
    oy = 1 - ylo
    xk = [lax.rem(x + o, 4) for o in OFFS]
    zk = [lax.rem(z + o, 4) for o in OFFS]
    x_peer = [at(x_=xk[k]) for k in range(3)]
    z_peer = [at(z_=zk[k]) for k in range(3)]
    y_peer = at(ylo_=oy)
    y_far = at(yhi_=1 - yhi, ylo_=oy)
    core_peer = at(core_=1 - core)
    rep_peers = [at(yhi_=1 - yhi), at(yhi_=1 - yhi, core_=1 - core), core_peer]

    half = pl.multiple_of(core * 64, 64)
    w_load = pltpu.make_async_copy(w_hbm.at[pl.ds(half, 64)], w, local_sem.at[0])
    cot_load = pltpu.make_async_copy(cot_hbm, cot, local_sem.at[1])
    mom_load = pltpu.make_async_copy(mom_hbm.at[0], mom, local_sem.at[2])
    tok_loads = []
    for k in range(4):
        cols = pl.ds(pl.multiple_of(xk[k] * 1024, 1024), 1024)
        tok_loads.append(pltpu.make_async_copy(tok_hbm.at[:, cols], tok.at[:, cols], local_sem.at[3 + k]))
    w_load.start()
    cot_load.start()
    for load in tok_loads:
        load.start()
    mom_load.start()
    small = [(kept_hbm, kept_ref), (rows_hbm, rows_ref), (fold_hbm, fold_ref)]
    small = [pltpu.make_async_copy(src, dst, local_sem.at[7 + i]) for i, (src, dst) in enumerate(small)]
    for load in small:
        load.start()

    barrier = pltpu.get_barrier_semaphore()
    everyone = x_peer + z_peer + [y_peer, y_far] + rep_peers
    for peer in everyone:
        pl.semaphore_signal(barrier, inc=1, device_id=peer, device_id_type=MESH)

    used = [0]
    sent = []

    def send(src, dst, peer, tag="rs"):
        n = used[0]
        used[0] += 1
        copy = pltpu.make_async_remote_copy(
            src_ref=src, dst_ref=dst, send_sem=send_sem.at[n], recv_sem=recv_sem.at[n],
            device_id=peer, device_id_type=MESH,
        )
        copy.start()
        sent.append(copy)
        return copy

    def same(view, peer, tag="ag"):
        return send(view, view, peer, tag)

    w_load.wait()
    rows_x, rows_z = pl.ds(half, 32), pl.ds(pl.multiple_of(half + 32, 32), 32)
    rows_c = pl.ds(half, 64)
    wf[x, z, ylo, rows_c] = w[...].astype(BF16)
    pl.semaphore_wait(barrier, len(everyone))
    gx = [same(wf.at[x, z, ylo, rows_x], peer) for peer in x_peer]
    gz = [same(wf.at[x, z, ylo, rows_z], peer) for peer in z_peer]
    far = [(same(wf.at[x, z, ylo, rows_c], y_far, "far"), wf.at[x, z, oy, rows_c])]

    cot_load.wait()
    y1 = []
    for k in range(4):
        xs = xk[k]
        tok_loads[k].wait()

        def block(zz, carry, xs=xs):
            cols = pl.ds(pl.multiple_of((xs * 4 + zz) * 256, 256), 256)
            part = lax.dot_general(
                tok[:, cols], cot[...], FROM_LEFT, preferred_element_type=F32
            ).astype(BF16)
            for p in range(8):
                parts[p, xs, zz, 0] = part[:128, p * WIDTH : p * WIDTH + WIDTH]
                parts[p, xs, zz, 1] = part[128:, p * WIDTH : p * WIDTH + WIDTH]
            return carry

        lax.fori_loop(0, 4, block, 0)
        y1.append([send(parts.at[p, xs, :, oy], got_y.at[p, xs], y_peer) for p in Y_PIECES])
        if k == 0:
            for copy in gx + gz:
                copy.wait_recv()
            hx, hz = [None] * 3, [None] * 3
            for i in (1, 2):
                hx[i] = same(wf.at[:, z, ylo, rows_x], z_peer[i])
                hz[i] = same(wf.at[x, :, ylo, rows_z], x_peer[i])
            for i in (1, 2, 0):
                far.append((same(wf.at[xk[i], z, ylo, rows_x], y_far, "far"), wf.at[xk[i], z, oy, rows_x]))
                far.append((same(wf.at[x, zk[i], ylo, rows_z], y_far, "far"), wf.at[x, zk[i], oy, rows_z]))

    def block_of(p, place, h):
        if p in X_PIECES:
            return parts.at[p, place, pl.ds(2 * h, 2)]
        return parts.at[p, pl.ds(2 * h, 2), place]

    def line(p):
        return (x, xk, x_peer) if p in X_PIECES else (z, zk, z_peer)

    s1 = {}

    def start_s1(p):
        _, places, peers = line(p)
        far_place, right, left = places[0], places[1], places[2]
        to_right, to_left = peers[1], peers[2]
        s1[p] = [
            send(block_of(p, far_place, 0), got_s1.at[p - 2, 0], to_right),
            send(block_of(p, far_place, 1), got_s1.at[p - 2, 1], to_left),
            send(block_of(p, right, 1), got_s1.at[p - 2, 2], to_right),
            send(block_of(p, left, 0), got_s1.at[p - 2, 3], to_left),
        ]

    def add_into(ref, sources, count):
        def one(i, carry):
            total = ref(i)[...].astype(F32)
            for source in sources:
                total += source(i)[...].astype(F32)
            ref(i)[...] = total.astype(BF16)
            return carry

        lax.fori_loop(0, count, one, 0)

    def chunk_of(p, place, h):
        if p in X_PIECES:
            return lambda c: parts.at[p, place, 2 * h + c // 2, c % 2]
        return lambda c: parts.at[p, 2 * h + c // 2, place, c % 2]

    def got(p, slot):
        return lambda c: got_s1.at[p - 2, slot, c // 2, c % 2]

    def pass_on(p):
        _, places, peers = line(p)
        right, left = places[1], places[2]
        s1[p][0].wait_recv()
        add_into(chunk_of(p, right, 0), [got(p, 0)], 4)
        s1[p].append(send(block_of(p, right, 0), got_s1.at[p - 2, 4], peers[1]))
        s1[p][1].wait_recv()
        add_into(chunk_of(p, left, 1), [got(p, 1)], 4)
        s1[p].append(send(block_of(p, left, 1), got_s1.at[p - 2, 5], peers[2]))

    def mine(p, c, y):
        if p in X_PIECES or p == Y_PIECES[0]:
            return parts.at[p, x, c, y]
        return parts.at[p, c, z, y]

    y2, last = {}, {}

    def finish_s1(p):
        place, _, _ = line(p)
        for copy in s1[p][2:]:
            copy.wait_recv()
        add_into(chunk_of(p, place, 0), [got(p, 3), got(p, 4)], 4)
        add_into(chunk_of(p, place, 1), [got(p, 2), got(p, 5)], 4)
        if p in X_PIECES:
            view = parts.at[p, x, :, oy]
        else:
            view = parts.at[p, :, z, oy]
        y2[p] = send(view, got_y2.at[p - 2], y_peer)

    def finish_y(p):
        y2[p].wait_recv()
        add_into(lambda c: mine(p, c, ylo), [lambda c: got_y2.at[p - 2, c]], 4)
        start_last(p)

    def start_last(p):
        peers, places = (z_peer, zk) if p in X_PIECES or p == Y_PIECES[0] else (x_peer, xk)
        last[p] = [send(mine(p, places[k], ylo), got_last.at[p, k], peers[k]) for k in range(3)]

    me = lax.axis_index("rep")

    def prepare():
        mom_load.wait()
        for load in small:
            load.wait()
        numbers[...] = kept_lanes(kept_ref[me])
        ex[me] = jnp.zeros((32, 128), F32)

    def finish(p):
        for copy in last[p]:
            copy.wait_recv()
        total = parts[p, x, z, ylo].astype(F32)
        for k in range(3):
            total += got_last[p, k].astype(F32)
        cols = slice(p * WIDTH, p * WIDTH + WIDTH)
        current = DECAY * mom[:, cols] + total * (1.0 / np.sqrt(24576.0))
        cur[:, cols] = current
        mid = dot_left(rows_ref[...], current)
        coefs = dot_right(mid, rows_ref[...], TURNED).reshape(2, 8, 8, WIDTH)
        places = block_numbers(WIDTH)
        masks = [
            [
                places == jnp.broadcast_to(numbers[2 * a + which, cols].reshape(1, 1, WIDTH), (8, 8, WIDTH))
                for a in range(2)
            ]
            for which in range(2)
        ]
        folded = [
            jnp.sum(jnp.where(masks[which][a], coefs[a], 0.0), axis=0) for which in range(2) for a in range(2)
        ]
        ex[me] += dot_marks(jnp.concatenate(folded, axis=0), fold_ref[cols])
        for a in range(2):
            kept_here = jnp.where(masks[0][a] | masks[1][a], coefs[a], 0.0)
            dense[a * 64 : a * 64 + 64, cols] = kept_here.reshape(64, WIDTH)

    def input_grad(plane, low, high):
        def one(i, carry):
            xx, zz = i // 2, (i % 2) * 2
            rows = jnp.concatenate([wf[xx, zz, plane], wf[xx, zz + 1, plane]], axis=0)
            out = lax.dot_general(cot[...], rows, TURNED, preferred_element_type=F32).astype(BF16)
            for j in range(2):
                cols = pl.ds(pl.multiple_of(((xx * 4 + zz + j) * 2 + plane) * 128, 128), 128)
                ig[:, cols] = out[:, j * 128 : j * 128 + 128]
            return carry

        lax.fori_loop(low, high, one, 0)

    onward = []
    for i in (1, 2):
        zs, xs = zk[3 - i], xk[3 - i]
        pair = pl.ds(2 * (i - 1), 2)
        hx[i].wait_recv()
        onward.append(same(wf.at[pair, zs, ylo, rows_x], z_peer[i]))
        far.append((same(wf.at[:, zs, ylo, rows_x], y_far, "far"), wf.at[:, zs, oy, rows_x]))
        hz[i].wait_recv()
        onward.append(same(wf.at[xs, pair, ylo, rows_z], x_peer[i]))
        far.append((same(wf.at[xs, :, ylo, rows_z], y_far, "far"), wf.at[xs, :, oy, rows_z]))
    for p in (2, 5, 3, 6):
        start_s1(p)
    pass_on(2)
    pass_on(5)
    start_s1(4)
    start_s1(7)
    for copy in onward:
        copy.wait_recv()
    far.append((same(wf.at[:, zk[0], ylo, rows_x], y_far, "far"), wf.at[:, zk[0], oy, rows_x]))
    far.append((same(wf.at[xk[0], :, ylo, rows_z], y_peer, "far"), wf.at[xk[0], :, oy, rows_z]))
    near = same(wf.at[:, :, ylo, rows_c], core_peer, "near")
    near.wait_recv()
    input_grad(ylo, 0, 8)
    pass_on(3)
    pass_on(6)

    prepare()
    for k in range(4):
        xs = xk[k]
        for p in Y_PIECES:
            y1[k][p].wait_recv()
            add_into(
                lambda c, p=p, xs=xs: parts.at[p, xs, c, ylo], [lambda c, p=p, xs=xs: got_y.at[p, xs, c]], 4
            )
    pass_on(4)
    pass_on(7)
    x2 = [send(parts.at[0, xk[k], :, ylo], got_x2.at[k], x_peer[k]) for k in range(3)]
    z2 = [send(parts.at[1, :, zk[k], ylo], got_z2.at[k], z_peer[k]) for k in range(3)]
    finish_s1(2)
    finish_s1(5)

    def forward(count):
        for copy, view in far[:count]:
            copy.wait_recv()
            near2.append(same(view, core_peer, "far"))
        del far[:count]

    near2 = []
    forward(7)
    finish_s1(3)
    finish_s1(6)
    finish_y(2)
    finish_y(5)
    finish_s1(4)
    finish_s1(7)
    for copy in x2:
        copy.wait_recv()
    add_into(lambda c: mine(0, c, ylo), [lambda c, k=k: got_x2.at[k, c] for k in range(3)], 4)
    start_last(0)
    for copy in z2:
        copy.wait_recv()
    add_into(lambda c: mine(1, c, ylo), [lambda c, k=k: got_z2.at[k, c] for k in range(3)], 4)
    start_last(1)
    finish_y(3)
    finish_y(6)
    forward(6)
    finish(2)
    finish(5)
    finish_y(4)
    finish_y(7)
    for copy in near2:
        copy.wait_recv()
    input_grad(oy, 0, 4)
    finish(3)
    finish(6)
    finish(0)
    finish(1)
    finish(4)
    finish(7)
    shared = [same(ex.at[me], peer, "ex") for peer in rep_peers]
    newmom[0] = cur[...] - from_coefs(dense[...], rows_ref[...])

    input_grad(oy, 4, 8)
    for copy in shared:
        copy.wait_recv()
    ex_out[...] = ex[...]
    for copy in sent:
        copy.wait_send()


def last_kernel(
    ig, mom, ex_ref, kept_ref, w_ref, rows_ref, fold_ref, ones_ref,
    ig_out, mom_out, neww_out, upd_out, neww_ref, upd_ref, sem,
):
    stores = [
        pltpu.make_async_copy(ig.at[pl.ds(i * 192, 192)], ig_out.at[pl.ds(i * 192, 192)], sem.at[i]) for i in range(4)
    ]
    stores.append(pltpu.make_async_copy(mom, mom_out, sem.at[4]))
    for store in stores:
        store.start()
    total = [jnp.zeros((8, 8, 1024), F32)] * 2
    wide = dot_marks(ex_ref[...].reshape(128, 128), fold_ref[...], TURNED).reshape(4, 2, 2, 8, 1024)
    numbers = kept_lanes(kept_ref[...].reshape(16, 16))
    places = block_numbers(1024)
    for r in range(4):
        for a in range(2):
            value = 0.0
            for which in (1, 0):
                at = r * 4 + a * 2 + which
                mask = places == jnp.broadcast_to(numbers[at : at + 1].reshape(1, 1, 1024), (8, 8, 1024))
                value = jnp.where(mask, jnp.broadcast_to(wide[r, which, a][None], (8, 8, 1024)), value)
            total[a] += value
    field = jnp.concatenate([t.reshape(64, 1024) for t in total], axis=0)
    average = from_coefs(field, rows_ref[...]) * 0.25
    squares = jnp.sum((average * average).reshape(2, 64, 1024), axis=1)
    means = dot_marks(side_by_side(squares, 128), ones_ref[...]) * (1.0 / (TILE * TILE))
    spread = jnp.sqrt(means + 1e-06)
    for i in range(8):
        for a in range(2):
            rows_a, cols = slice(a * 64, a * 64 + 64), slice(i * 128, i * 128 + 128)
            avg = average[rows_a, cols]
            update = avg / (jnp.abs(avg) + spread[i * 2 + a : i * 2 + a + 1])
            upd_ref[rows_a, cols] = update
            neww_ref[rows_a, cols] = w_ref[rows_a, cols] - STEP * update
    results = [(neww_ref, neww_out), (upd_ref, upd_out)]
    results = [pltpu.make_async_copy(src, dst, sem.at[5 + i]) for i, (src, dst) in enumerate(results)]
    for store in results:
        store.start()
    for store in stores + results:
        store.wait()


def body(tokens, cotangent, weight, momentum, kept):
    vmem = pl.BlockSpec(memory_space=pltpu.VMEM)
    any_space = pl.BlockSpec(memory_space=pl.ANY)
    rows, fold = jnp.asarray(two_halves(dct_matrix(2))), jnp.asarray(fold_matrix())
    ones = jnp.asarray(np.kron(np.eye(2), np.ones((TILE, TILE))).astype(jnp.bfloat16))
    kept = kept.transpose(0, 1, 3, 2).reshape(4, 4, 16)
    constants = [
        pltpu.VMEM((4, 4, 16), jnp.int32),
        pltpu.VMEM((2, 128, 128), BF16),
        pltpu.VMEM((1024, 128), BF16),
    ]
    sems = 160
    between = pl.pallas_call(
        main_kernel,
        out_shape=(
            pltpu.VMEM((768, 4096), BF16),
            pltpu.VMEM((1, 128, 1024), F32),
            pltpu.VMEM((4, 32, 128), F32),
        ),
        in_specs=[any_space] * 7,
        out_specs=(vmem, vmem, vmem),
        scratch_shapes=[
            pltpu.VMEM((768, 4096), BF16),
            pltpu.VMEM((768, 1024), BF16),
            pltpu.VMEM((64, 1024), F32),
            pltpu.VMEM((128, 1024), F32),
            *constants,
            pltpu.VMEM((4, 4, 2, 128, 1024), BF16),
            pltpu.VMEM((8, 4, 4, 2, 128, WIDTH), BF16),
            pltpu.VMEM((2, 4, 4, 128, WIDTH), BF16),
            pltpu.VMEM((6, 6, 2, 2, 128, WIDTH), BF16),
            pltpu.VMEM((3, 4, 128, WIDTH), BF16),
            pltpu.VMEM((3, 4, 128, WIDTH), BF16),
            pltpu.VMEM((6, 4, 128, WIDTH), BF16),
            pltpu.VMEM((8, 3, 128, WIDTH), BF16),
            pltpu.VMEM((128, 1024), F32),
            pltpu.VMEM((128, 1024), F32),
            pltpu.VMEM((4, 1024), F32),
            pltpu.VMEM((4, 32, 128), F32),
            pltpu.SemaphoreType.DMA((10,)),
            pltpu.SemaphoreType.DMA((sems,)),
            pltpu.SemaphoreType.DMA((sems,)),
        ],
        compiler_params=pltpu.CompilerParams(
            collective_id=0, has_side_effects=True, vmem_limit_bytes=48 << 20
        ),
        cost_estimate=pl.CostEstimate(flops=13 * 10**9, bytes_accessed=20 * 10**6, transcendentals=0),
        name="gradients",
    )(tokens, cotangent, weight, momentum, kept, rows, fold)
    between = [pltpu.with_memory_space_constraint(a, pltpu.VMEM) for a in between]
    return pl.pallas_call(
        last_kernel,
        out_shape=(
            jax.ShapeDtypeStruct((768, 4096), BF16),
            jax.ShapeDtypeStruct((1, 128, 1024), F32),
            jax.ShapeDtypeStruct((128, 1024), F32),
            jax.ShapeDtypeStruct((128, 1024), F32),
        ),
        in_specs=[vmem] * 8,
        out_specs=(any_space, any_space, any_space, any_space),
        scratch_shapes=[
            pltpu.VMEM((128, 1024), F32),
            pltpu.VMEM((128, 1024), F32),
            pltpu.SemaphoreType.DMA((7,)),
        ],
        compiler_params=pltpu.CompilerParams(vmem_limit_bytes=40 << 20),
        name="step",
    )(*between, kept, weight, rows, fold, ones)


def solution(mesh):
    in_specs = (
        P(("rep", "fsdp"), None),
        P(("rep", "fsdp"), None),
        P("fsdp", None),
        P("rep", "fsdp", None),
        P(None, "fsdp", None, None),
    )
    out_specs = (P(("rep", "fsdp"), None), P("rep", "fsdp", None), P("fsdp", None), P("fsdp", None))
    return jax.shard_map(body, mesh=mesh, in_specs=in_specs, out_specs=out_specs, check_vma=False)
```

```python
import jax
import jax.numpy as jnp
import numpy as np
from jax import lax
from jax.experimental import pallas as pl
from jax.experimental.pallas import tpu as pltpu
from jax.sharding import PartitionSpec as P

TILE = 64
BLK = 8
DECAY = 0.999
STEP = 0.02
MESH = pl.DeviceIdType.MESH
F32 = jnp.float32
BF16 = jnp.bfloat16

WIDTH = 128
Y_PIECES, X_PIECES, Z_PIECES = (0, 1), (2, 3, 4), (5, 6, 7)
OFFS = (2, 1, 3, 0)


def dct_matrix(copies):
    freq = np.arange(TILE, dtype=np.float64)[:, None]
    place = np.arange(TILE, dtype=np.float64)[None, :]
    table = np.cos(np.pi * (2.0 * place + 1.0) * freq / (2.0 * TILE))
    table *= np.where(freq == 0.0, np.sqrt(1.0 / TILE), np.sqrt(2.0 / TILE))
    return np.kron(np.eye(copies), table).astype(np.float32)


def two_halves(matrix):
    high = matrix.astype(jnp.bfloat16)
    low = (matrix - high.astype(np.float32)).astype(jnp.bfloat16)
    return np.stack([high, low])


def fold_matrix():
    fold = np.zeros((1024, 128), np.float32)
    lane = np.arange(1024)
    fold[lane, (lane // TILE) * BLK + lane % BLK] = 1.0
    return fold.astype(jnp.bfloat16)


PLAIN = (((1,), (0,)), ((), ()))
TURNED = (((1,), (1,)), ((), ()))
FROM_LEFT = (((0,), (0,)), ((), ()))


def dot(a, b, dims=PLAIN):
    return lax.dot_general(a, b, dims, preferred_element_type=F32)


def halves(a):
    high = a.astype(BF16)
    return high, (a - high.astype(F32)).astype(BF16)


def dot_marks(a, marks, dims=PLAIN):
    count = a.shape[0]
    high = a.astype(BF16)
    rest = a - high.astype(F32)
    mid = rest.astype(BF16)
    low = (rest - mid.astype(F32)).astype(BF16)
    out = dot(jnp.concatenate([high, mid, low], axis=0), marks, dims)
    return out[:count] + (out[count : 2 * count] + out[2 * count :])


def dot_left(table, field, dims=PLAIN):
    high, low = halves(field)
    if dims is FROM_LEFT:
        return dot(table[0], high, dims) + (dot(table[0], low, dims) + dot(table[1], high, dims))
    count = table.shape[1]
    out = dot(table.reshape(2 * count, count), high, dims)
    return out[:count] + (out[count:] + dot(table[0], low, dims))


def dot_right(field, table, dims=PLAIN):
    count = field.shape[0]
    high, low = halves(field)
    out = dot(jnp.concatenate([high, low], axis=0), table[0], dims)
    return out[:count] + (out[count:] + dot(high, table[1], dims))


def side_by_side(field, width):
    return jnp.concatenate([field[:, i : i + width] for i in range(0, 1024, width)], axis=0)


def from_coefs(coefs, rows):
    count = coefs.shape[0]
    none = jnp.zeros((128, 128), BF16)
    lanes = [
        jnp.concatenate([jnp.concatenate([r, none], axis=1), jnp.concatenate([none, r], axis=1)], axis=0)
        for r in (rows[0], rows[1])
    ]
    mid = side_by_side(dot_left(rows, coefs, FROM_LEFT), 256)
    out = dot_right(mid, lanes)
    return jnp.concatenate([out[i * count : i * count + count] for i in range(4)], axis=1)


def block_numbers(width):
    number = lax.broadcasted_iota(jnp.int32, (8, 8, width), 0) * 8 + (
        lax.broadcasted_iota(jnp.int32, (8, 8, width), 2) % TILE
    ) // BLK
    return number.astype(F32)


def kept_lanes(kept):
    tile = lax.broadcasted_iota(jnp.int32, (16, 1024), 0)
    marks = jnp.where(tile == lax.broadcasted_iota(jnp.int32, (16, 1024), 1) // TILE, 1.0, 0.0)
    return dot(kept.astype(F32).astype(BF16), marks.astype(BF16))


def make_places():
    rep, shard = lax.axis_index("rep"), lax.axis_index("fsdp")
    yhi, core = rep // 2, rep % 2
    x, z, ylo = shard // 8, (shard // 2) % 4, shard % 2

    def at(yhi_=None, core_=None, x_=None, z_=None, ylo_=None):
        h = yhi if yhi_ is None else yhi_
        c = core if core_ is None else core_
        xx = x if x_ is None else x_
        zz = z if z_ is None else z_
        l = ylo if ylo_ is None else ylo_
        return (h * 2 + c, (xx * 4 + zz) * 2 + l)

    return yhi, core, x, z, ylo, at


def main_kernel(
    tok_hbm, cot_hbm, w_hbm, mom_hbm, kept_hbm, rows_hbm, fold_hbm,
    ig, newmom, ex_out,
    tok, cot, w, mom, kept_ref, rows_ref, fold_ref,
    wf, parts, got_y, got_s1, got_x2, got_z2, got_y2, got_last,
    cur, dense, numbers, ex, local_sem, send_sem, recv_sem,
):
    yhi, core, x, z, ylo, at = make_places()
    oy = 1 - ylo
    xk = [lax.rem(x + o, 4) for o in OFFS]
    zk = [lax.rem(z + o, 4) for o in OFFS]
    x_peer = [at(x_=xk[k]) for k in range(3)]
    z_peer = [at(z_=zk[k]) for k in range(3)]
    y_peer = at(ylo_=oy)
    y_far = at(yhi_=1 - yhi, ylo_=oy)
    core_peer = at(core_=1 - core)
    rep_peers = [at(yhi_=1 - yhi), at(yhi_=1 - yhi, core_=1 - core), core_peer]

    half = pl.multiple_of(core * 64, 64)
    w_load = pltpu.make_async_copy(w_hbm.at[pl.ds(half, 64)], w, local_sem.at[0])
    cot_load = pltpu.make_async_copy(cot_hbm, cot, local_sem.at[1])
    mom_load = pltpu.make_async_copy(mom_hbm.at[0], mom, local_sem.at[2])
    tok_loads = []
    for k in range(4):
        cols = pl.ds(pl.multiple_of(xk[k] * 1024, 1024), 1024)
        tok_loads.append(pltpu.make_async_copy(tok_hbm.at[:, cols], tok.at[:, cols], local_sem.at[3 + k]))
    w_load.start()
    cot_load.start()
    for load in tok_loads:
        load.start()
    mom_load.start()
    small = [(kept_hbm, kept_ref), (rows_hbm, rows_ref), (fold_hbm, fold_ref)]
    small = [pltpu.make_async_copy(src, dst, local_sem.at[7 + i]) for i, (src, dst) in enumerate(small)]
    for load in small:
        load.start()

    barrier = pltpu.get_barrier_semaphore()
    everyone = x_peer + z_peer + [y_peer, y_far] + rep_peers
    for peer in everyone:
        pl.semaphore_signal(barrier, inc=1, device_id=peer, device_id_type=MESH)

    used = [0]
    sent = []

    def send(src, dst, peer, tag="rs"):
        n = used[0]
        used[0] += 1
        copy = pltpu.make_async_remote_copy(
            src_ref=src, dst_ref=dst, send_sem=send_sem.at[n], recv_sem=recv_sem.at[n],
            device_id=peer, device_id_type=MESH,
        )
        copy.start()
        sent.append(copy)
        return copy

    def same(view, peer, tag="ag"):
        return send(view, view, peer, tag)

    w_load.wait()
    rows_x, rows_z = pl.ds(half, 32), pl.ds(pl.multiple_of(half + 32, 32), 32)
    rows_c = pl.ds(half, 64)
    wf[x, z, ylo, rows_c] = w[...].astype(BF16)
    pl.semaphore_wait(barrier, len(everyone))
    gx = [same(wf.at[x, z, ylo, rows_x], peer) for peer in x_peer]
    gz = [same(wf.at[x, z, ylo, rows_z], peer) for peer in z_peer]
    far = [(same(wf.at[x, z, ylo, rows_c], y_far, "far"), wf.at[x, z, oy, rows_c])]

    cot_load.wait()
    y1 = []
    for k in range(4):
        xs = xk[k]
        tok_loads[k].wait()

        def block(zz, carry, xs=xs):
            cols = pl.ds(pl.multiple_of((xs * 4 + zz * 2) * 256, 512), 512)
            part = lax.dot_general(
                tok[:, cols], cot[...], FROM_LEFT, preferred_element_type=F32
            ).astype(BF16)
            for p in range(8):
                for q in range(4):
                    chunk = part[q * 128 : q * 128 + 128, p * WIDTH : p * WIDTH + WIDTH]
                    parts[p, xs, zz * 2 + q // 2, q % 2] = chunk
            return carry

        lax.fori_loop(0, 2, block, 0)
        y1.append([send(parts.at[p, xs, :, oy], got_y.at[p, xs], y_peer) for p in Y_PIECES])
        if k == 0:
            for copy in gx + gz:
                copy.wait_recv()
            hx, hz = [None] * 3, [None] * 3
            for i in (1, 2):
                hx[i] = same(wf.at[:, z, ylo, rows_x], z_peer[i])
                hz[i] = same(wf.at[x, :, ylo, rows_z], x_peer[i])
            for i in (1, 2, 0):
                far.append((same(wf.at[xk[i], z, ylo, rows_x], y_far, "far"), wf.at[xk[i], z, oy, rows_x]))
                far.append((same(wf.at[x, zk[i], ylo, rows_z], y_far, "far"), wf.at[x, zk[i], oy, rows_z]))

    def block_of(p, place, h):
        if p in X_PIECES:
            return parts.at[p, place, pl.ds(2 * h, 2)]
        return parts.at[p, pl.ds(2 * h, 2), place]

    def line(p):
        return (x, xk, x_peer) if p in X_PIECES else (z, zk, z_peer)

    s1 = {}

    def start_s1(p):
        _, places, peers = line(p)
        far_place, right, left = places[0], places[1], places[2]
        to_right, to_left = peers[1], peers[2]
        s1[p] = [
            send(block_of(p, far_place, 0), got_s1.at[p - 2, 0], to_right),
            send(block_of(p, far_place, 1), got_s1.at[p - 2, 1], to_left),
            send(block_of(p, right, 1), got_s1.at[p - 2, 2], to_right),
            send(block_of(p, left, 0), got_s1.at[p - 2, 3], to_left),
        ]

    def add_into(ref, sources, count):
        def one(i, carry):
            total = ref(i)[...].astype(F32)
            for source in sources:
                total += source(i)[...].astype(F32)
            ref(i)[...] = total.astype(BF16)
            return carry

        lax.fori_loop(0, count, one, 0)

    def chunk_of(p, place, h):
        if p in X_PIECES:
            return lambda c: parts.at[p, place, 2 * h + c // 2, c % 2]
        return lambda c: parts.at[p, 2 * h + c // 2, place, c % 2]

    def got(p, slot):
        return lambda c: got_s1.at[p - 2, slot, c // 2, c % 2]

    def pass_on(p):
        _, places, peers = line(p)
        right, left = places[1], places[2]
        s1[p][0].wait_recv()
        add_into(chunk_of(p, right, 0), [got(p, 0)], 4)
        s1[p].append(send(block_of(p, right, 0), got_s1.at[p - 2, 4], peers[1]))
        s1[p][1].wait_recv()
        add_into(chunk_of(p, left, 1), [got(p, 1)], 4)
        s1[p].append(send(block_of(p, left, 1), got_s1.at[p - 2, 5], peers[2]))

    def mine(p, c, y):
        if p in X_PIECES or p == Y_PIECES[0]:
            return parts.at[p, x, c, y]
        return parts.at[p, c, z, y]

    y2, last = {}, {}

    def finish_s1(p):
        place, _, _ = line(p)
        for copy in s1[p][2:]:
            copy.wait_recv()
        add_into(chunk_of(p, place, 0), [got(p, 3), got(p, 4)], 4)
        add_into(chunk_of(p, place, 1), [got(p, 2), got(p, 5)], 4)
        if p in X_PIECES:
            view = parts.at[p, x, :, oy]
        else:
            view = parts.at[p, :, z, oy]
        y2[p] = send(view, got_y2.at[p - 2], y_peer)

    def finish_y(p):
        y2[p].wait_recv()
        add_into(lambda c: mine(p, c, ylo), [lambda c: got_y2.at[p - 2, c]], 4)
        start_last(p)

    def start_last(p):
        peers, places = (z_peer, zk) if p in X_PIECES or p == Y_PIECES[0] else (x_peer, xk)
        last[p] = [send(mine(p, places[k], ylo), got_last.at[p, k], peers[k]) for k in range(3)]

    me = lax.axis_index("rep")

    def prepare():
        mom_load.wait()
        for load in small:
            load.wait()
        numbers[...] = kept_lanes(kept_ref[me])
        ex[me] = jnp.zeros((32, 128), F32)

    def finish(*pieces):
        fields = []
        for p in pieces:
            for copy in last[p]:
                copy.wait_recv()
            total = parts[p, x, z, ylo].astype(F32)
            for k in range(3):
                total += got_last[p, k].astype(F32)
            cols = slice(p * WIDTH, p * WIDTH + WIDTH)
            current = DECAY * mom[:, cols] + total * (1.0 / np.sqrt(24576.0))
            cur[:, cols] = current
            fields.append(current)
        mid = dot_left(rows_ref[...], jnp.concatenate(fields, axis=1))
        mid = jnp.concatenate([mid[:, i * WIDTH : i * WIDTH + WIDTH] for i in range(len(pieces))], axis=0)
        coefs_all = dot_right(mid, rows_ref[...], TURNED)
        places = block_numbers(WIDTH)
        shares = []
        for i, p in enumerate(pieces):
            coefs = coefs_all[i * 128 : i * 128 + 128].reshape(2, 8, 8, WIDTH)
            cols = slice(p * WIDTH, p * WIDTH + WIDTH)
            masks = [
                [
                    places == jnp.broadcast_to(numbers[2 * a + which, cols].reshape(1, 1, WIDTH), (8, 8, WIDTH))
                    for a in range(2)
                ]
                for which in range(2)
            ]
            folded = [
                jnp.sum(jnp.where(masks[which][a], coefs[a], 0.0), axis=0) for which in range(2) for a in range(2)
            ]
            shares.append(dot_marks(jnp.concatenate(folded, axis=0), fold_ref[cols]))
            for a in range(2):
                kept_here = jnp.where(masks[0][a] | masks[1][a], coefs[a], 0.0)
                dense[a * 64 : a * 64 + 64, cols] = kept_here.reshape(64, WIDTH)
        ex[me] += sum(shares[1:], shares[0])

    def input_grad(plane, low, high):
        def one(i, carry):
            xx, zz = i // 2, (i % 2) * 2
            rows = jnp.concatenate([wf[xx, zz, plane], wf[xx, zz + 1, plane]], axis=0)
            out = lax.dot_general(cot[...], rows, TURNED, preferred_element_type=F32).astype(BF16)
            for j in range(2):
                cols = pl.ds(pl.multiple_of(((xx * 4 + zz + j) * 2 + plane) * 128, 128), 128)
                ig[:, cols] = out[:, j * 128 : j * 128 + 128]
            return carry

        lax.fori_loop(low, high, one, 0)

    onward = []
    for i in (1, 2):
        zs, xs = zk[3 - i], xk[3 - i]
        pair = pl.ds(2 * (i - 1), 2)
        hx[i].wait_recv()
        onward.append(same(wf.at[pair, zs, ylo, rows_x], z_peer[i]))
        far.append((same(wf.at[:, zs, ylo, rows_x], y_far, "far"), wf.at[:, zs, oy, rows_x]))
        hz[i].wait_recv()
        onward.append(same(wf.at[xs, pair, ylo, rows_z], x_peer[i]))
        far.append((same(wf.at[xs, :, ylo, rows_z], y_far, "far"), wf.at[xs, :, oy, rows_z]))
    for p in (2, 5, 3, 6):
        start_s1(p)
    pass_on(2)
    pass_on(5)
    start_s1(4)
    start_s1(7)
    for copy in onward:
        copy.wait_recv()
    far.append((same(wf.at[:, zk[0], ylo, rows_x], y_far, "far"), wf.at[:, zk[0], oy, rows_x]))
    far.append((same(wf.at[xk[0], :, ylo, rows_z], y_peer, "far"), wf.at[xk[0], :, oy, rows_z]))
    near = same(wf.at[:, :, ylo, rows_c], core_peer, "near")
    near.wait_recv()
    input_grad(ylo, 0, 8)
    pass_on(3)
    pass_on(6)

    prepare()
    for k in range(4):
        xs = xk[k]
        for p in Y_PIECES:
            y1[k][p].wait_recv()
            add_into(
                lambda c, p=p, xs=xs: parts.at[p, xs, c, ylo], [lambda c, p=p, xs=xs: got_y.at[p, xs, c]], 4
            )
    pass_on(4)
    pass_on(7)
    x2 = [send(parts.at[0, xk[k], :, ylo], got_x2.at[k], x_peer[k]) for k in range(3)]
    z2 = [send(parts.at[1, :, zk[k], ylo], got_z2.at[k], z_peer[k]) for k in range(3)]
    finish_s1(2)
    finish_s1(5)

    def forward(count):
        for copy, view in far[:count]:
            copy.wait_recv()
            near2.append(same(view, core_peer, "far"))
        del far[:count]

    near2 = []
    forward(7)
    finish_s1(3)
    finish_s1(6)
    finish_y(2)
    finish_y(5)
    finish_s1(4)
    finish_s1(7)
    for copy in x2:
        copy.wait_recv()
    add_into(lambda c: mine(0, c, ylo), [lambda c, k=k: got_x2.at[k, c] for k in range(3)], 4)
    start_last(0)
    for copy in z2:
        copy.wait_recv()
    add_into(lambda c: mine(1, c, ylo), [lambda c, k=k: got_z2.at[k, c] for k in range(3)], 4)
    start_last(1)
    finish_y(3)
    finish_y(6)
    forward(6)
    finish(2, 5)
    finish_y(4)
    finish_y(7)
    for copy in near2:
        copy.wait_recv()
    input_grad(oy, 0, 4)
    finish(3, 6)
    finish(0, 1)
    finish(4, 7)
    shared = [same(ex.at[me], peer, "ex") for peer in rep_peers]
    newmom[0] = cur[...] - from_coefs(dense[...], rows_ref[...])

    input_grad(oy, 4, 8)
    for copy in shared:
        copy.wait_recv()
    ex_out[...] = ex[...]
    for copy in sent:
        copy.wait_send()


def last_kernel(
    ig, mom, ex_ref, kept_hbm, w_hbm, rows_hbm, fold_hbm, ones_hbm,
    ig_out, mom_out, neww_out, upd_out,
    w_ref, kept_ref, rows_ref, fold_ref, ones_ref, neww_ref, upd_ref, sem,
):
    small = [(kept_hbm, kept_ref), (fold_hbm, fold_ref), (rows_hbm, rows_ref), (ones_hbm, ones_ref), (w_hbm, w_ref)]
    small = [pltpu.make_async_copy(src, dst, sem.at[7 + i]) for i, (src, dst) in enumerate(small)]
    for load in small:
        load.start()
    stores = [
        pltpu.make_async_copy(ig.at[pl.ds(i * 192, 192)], ig_out.at[pl.ds(i * 192, 192)], sem.at[i]) for i in range(4)
    ]
    stores.append(pltpu.make_async_copy(mom, mom_out, sem.at[4]))
    for store in stores:
        store.start()
    for load in small:
        load.wait()
    total = [jnp.zeros((8, 8, 1024), F32)] * 2
    wide = dot_marks(ex_ref[...].reshape(128, 128), fold_ref[...], TURNED).reshape(4, 2, 2, 8, 1024)
    numbers = kept_lanes(kept_ref[...].reshape(16, 16))
    places = block_numbers(1024)
    for r in range(4):
        for a in range(2):
            value = 0.0
            for which in (1, 0):
                at = r * 4 + a * 2 + which
                mask = places == jnp.broadcast_to(numbers[at : at + 1].reshape(1, 1, 1024), (8, 8, 1024))
                value = jnp.where(mask, jnp.broadcast_to(wide[r, which, a][None], (8, 8, 1024)), value)
            total[a] += value
    field = jnp.concatenate([t.reshape(64, 1024) for t in total], axis=0)
    average = from_coefs(field, rows_ref[...]) * 0.25
    squares = jnp.sum((average * average).reshape(2, 64, 1024), axis=1)
    means = dot_marks(side_by_side(squares, 128), ones_ref[...]) * (1.0 / (TILE * TILE))
    spread = jnp.sqrt(means + 1e-06)
    for i in range(8):
        for a in range(2):
            rows_a, cols = slice(a * 64, a * 64 + 64), slice(i * 128, i * 128 + 128)
            avg = average[rows_a, cols]
            update = avg / (jnp.abs(avg) + spread[i * 2 + a : i * 2 + a + 1])
            upd_ref[rows_a, cols] = update
            neww_ref[rows_a, cols] = w_ref[rows_a, cols] - STEP * update
    results = [(neww_ref, neww_out), (upd_ref, upd_out)]
    results = [pltpu.make_async_copy(src, dst, sem.at[5 + i]) for i, (src, dst) in enumerate(results)]
    for store in results:
        store.start()
    for store in stores + results:
        store.wait()


def body(tokens, cotangent, weight, momentum, kept):
    vmem = pl.BlockSpec(memory_space=pltpu.VMEM)
    any_space = pl.BlockSpec(memory_space=pl.ANY)
    rows, fold = jnp.asarray(two_halves(dct_matrix(2))), jnp.asarray(fold_matrix())
    ones = jnp.asarray(np.kron(np.eye(2), np.ones((TILE, TILE))).astype(jnp.bfloat16))
    kept = kept.transpose(0, 1, 3, 2).reshape(4, 4, 16)
    constants = [
        pltpu.VMEM((4, 4, 16), jnp.int32),
        pltpu.VMEM((2, 128, 128), BF16),
        pltpu.VMEM((1024, 128), BF16),
    ]
    sems = 160
    between = pl.pallas_call(
        main_kernel,
        out_shape=(
            pltpu.VMEM((768, 4096), BF16),
            pltpu.VMEM((1, 128, 1024), F32),
            pltpu.VMEM((4, 32, 128), F32),
        ),
        in_specs=[any_space] * 7,
        out_specs=(vmem, vmem, vmem),
        scratch_shapes=[
            pltpu.VMEM((768, 4096), BF16),
            pltpu.VMEM((768, 1024), BF16),
            pltpu.VMEM((64, 1024), F32),
            pltpu.VMEM((128, 1024), F32),
            *constants,
            pltpu.VMEM((4, 4, 2, 128, 1024), BF16),
            pltpu.VMEM((8, 4, 4, 2, 128, WIDTH), BF16),
            pltpu.VMEM((2, 4, 4, 128, WIDTH), BF16),
            pltpu.VMEM((6, 6, 2, 2, 128, WIDTH), BF16),
            pltpu.VMEM((3, 4, 128, WIDTH), BF16),
            pltpu.VMEM((3, 4, 128, WIDTH), BF16),
            pltpu.VMEM((6, 4, 128, WIDTH), BF16),
            pltpu.VMEM((8, 3, 128, WIDTH), BF16),
            pltpu.VMEM((128, 1024), F32),
            pltpu.VMEM((128, 1024), F32),
            pltpu.VMEM((4, 1024), F32),
            pltpu.VMEM((4, 32, 128), F32),
            pltpu.SemaphoreType.DMA((10,)),
            pltpu.SemaphoreType.DMA((sems,)),
            pltpu.SemaphoreType.DMA((sems,)),
        ],
        compiler_params=pltpu.CompilerParams(
            collective_id=0, has_side_effects=True, vmem_limit_bytes=48 << 20
        ),
        cost_estimate=pl.CostEstimate(flops=13 * 10**9, bytes_accessed=20 * 10**6, transcendentals=0),
        name="gradients",
    )(tokens, cotangent, weight, momentum, kept, rows, fold)
    between = [pltpu.with_memory_space_constraint(a, pltpu.VMEM) for a in between]
    return pl.pallas_call(
        last_kernel,
        out_shape=(
            jax.ShapeDtypeStruct((768, 4096), BF16),
            jax.ShapeDtypeStruct((1, 128, 1024), F32),
            jax.ShapeDtypeStruct((128, 1024), F32),
            jax.ShapeDtypeStruct((128, 1024), F32),
        ),
        in_specs=[vmem] * 3 + [any_space] * 5,
        out_specs=(any_space, any_space, any_space, any_space),
        scratch_shapes=[
            pltpu.VMEM((128, 1024), F32),
            *constants,
            pltpu.VMEM((128, 128), BF16),
            pltpu.VMEM((128, 1024), F32),
            pltpu.VMEM((128, 1024), F32),
            pltpu.SemaphoreType.DMA((12,)),
        ],
        compiler_params=pltpu.CompilerParams(vmem_limit_bytes=40 << 20),
        name="step",
    )(*between, kept, weight, rows, fold, ones)


def solution(mesh):
    in_specs = (
        P(("rep", "fsdp"), None),
        P(("rep", "fsdp"), None),
        P("fsdp", None),
        P("rep", "fsdp", None),
        P(None, "fsdp", None, None),
    )
    out_specs = (P(("rep", "fsdp"), None), P("rep", "fsdp", None), P("fsdp", None), P("fsdp", None))
    return jax.shard_map(body, mesh=mesh, in_specs=in_specs, out_specs=out_specs, check_vma=False)
```

```python
import jax
import jax.numpy as jnp
import numpy as np
from jax import lax
from jax.experimental import pallas as pl
from jax.experimental.pallas import tpu as pltpu
from jax.sharding import PartitionSpec as P

TILE = 64
BLK = 8
DECAY = 0.999
STEP = 0.02
MESH = pl.DeviceIdType.MESH
F32 = jnp.float32
BF16 = jnp.bfloat16

WIDTH = 128
Y_PIECES, X_PIECES, Z_PIECES = (0, 1), (2, 3, 4), (5, 6, 7)
OFFS = (2, 1, 3, 0)


def dct_matrix(copies):
    freq = np.arange(TILE, dtype=np.float64)[:, None]
    place = np.arange(TILE, dtype=np.float64)[None, :]
    table = np.cos(np.pi * (2.0 * place + 1.0) * freq / (2.0 * TILE))
    table *= np.where(freq == 0.0, np.sqrt(1.0 / TILE), np.sqrt(2.0 / TILE))
    return np.kron(np.eye(copies), table).astype(np.float32)


def two_halves(matrix):
    high = matrix.astype(jnp.bfloat16)
    low = (matrix - high.astype(np.float32)).astype(jnp.bfloat16)
    return np.stack([high, low])


def fold_matrix():
    fold = np.zeros((1024, 128), np.float32)
    lane = np.arange(1024)
    fold[lane, (lane // TILE) * BLK + lane % BLK] = 1.0
    return fold.astype(jnp.bfloat16)


PLAIN = (((1,), (0,)), ((), ()))
TURNED = (((1,), (1,)), ((), ()))
FROM_LEFT = (((0,), (0,)), ((), ()))


def dot(a, b, dims=PLAIN):
    return lax.dot_general(a, b, dims, preferred_element_type=F32)


def halves(a):
    high = a.astype(BF16)
    return high, (a - high.astype(F32)).astype(BF16)


def dot_marks(a, marks, dims=PLAIN):
    count = a.shape[0]
    high = a.astype(BF16)
    rest = a - high.astype(F32)
    mid = rest.astype(BF16)
    low = (rest - mid.astype(F32)).astype(BF16)
    out = dot(jnp.concatenate([high, mid, low], axis=0), marks, dims)
    return out[:count] + (out[count : 2 * count] + out[2 * count :])


def dot_left(table, field, dims=PLAIN):
    high, low = halves(field)
    if dims is FROM_LEFT:
        return dot(table[0], high, dims) + (dot(table[0], low, dims) + dot(table[1], high, dims))
    count = table.shape[1]
    out = dot(table.reshape(2 * count, count), high, dims)
    return out[:count] + (out[count:] + dot(table[0], low, dims))


def dot_right(field, table, dims=PLAIN):
    count = field.shape[0]
    high, low = halves(field)
    out = dot(jnp.concatenate([high, low], axis=0), table[0], dims)
    return out[:count] + (out[count:] + dot(high, table[1], dims))


def side_by_side(field, width):
    return jnp.concatenate([field[:, i : i + width] for i in range(0, 1024, width)], axis=0)


def from_coefs(coefs, rows):
    count = coefs.shape[0]
    none = jnp.zeros((128, 128), BF16)
    lanes = [
        jnp.concatenate([jnp.concatenate([r, none], axis=1), jnp.concatenate([none, r], axis=1)], axis=0)
        for r in (rows[0], rows[1])
    ]
    mid = side_by_side(dot_left(rows, coefs, FROM_LEFT), 256)
    out = dot_right(mid, lanes)
    return jnp.concatenate([out[i * count : i * count + count] for i in range(4)], axis=1)


def block_numbers(width):
    number = lax.broadcasted_iota(jnp.int32, (8, 8, width), 0) * 8 + (
        lax.broadcasted_iota(jnp.int32, (8, 8, width), 2) % TILE
    ) // BLK
    return number.astype(F32)


def kept_lanes(kept):
    tile = lax.broadcasted_iota(jnp.int32, (16, 1024), 0)
    marks = jnp.where(tile == lax.broadcasted_iota(jnp.int32, (16, 1024), 1) // TILE, 1.0, 0.0)
    return dot(kept.astype(F32).astype(BF16), marks.astype(BF16))


def make_places():
    rep, shard = lax.axis_index("rep"), lax.axis_index("fsdp")
    yhi, core = rep // 2, rep % 2
    x, z, ylo = shard // 8, (shard // 2) % 4, shard % 2

    def at(yhi_=None, core_=None, x_=None, z_=None, ylo_=None):
        h = yhi if yhi_ is None else yhi_
        c = core if core_ is None else core_
        xx = x if x_ is None else x_
        zz = z if z_ is None else z_
        l = ylo if ylo_ is None else ylo_
        return (h * 2 + c, (xx * 4 + zz) * 2 + l)

    return yhi, core, x, z, ylo, at


def main_kernel(
    tok_hbm, cot_hbm, w_hbm, mom_hbm, kept_hbm, rows_hbm, fold_hbm,
    ig, newmom, ex_out,
    tok, cot, w, mom, kept_ref, rows_ref, fold_ref,
    wf, parts, got_y, got_s1, got_x2, got_z2, got_y2, got_last,
    cur, dense, numbers, ex, local_sem, send_sem, recv_sem,
):
    yhi, core, x, z, ylo, at = make_places()
    oy = 1 - ylo
    xk = [lax.rem(x + o, 4) for o in OFFS]
    zk = [lax.rem(z + o, 4) for o in OFFS]
    x_peer = [at(x_=xk[k]) for k in range(3)]
    z_peer = [at(z_=zk[k]) for k in range(3)]
    y_peer = at(ylo_=oy)
    y_far = at(yhi_=1 - yhi, ylo_=oy)
    core_peer = at(core_=1 - core)
    rep_peers = [at(yhi_=1 - yhi), at(yhi_=1 - yhi, core_=1 - core), core_peer]

    half = pl.multiple_of(core * 64, 64)
    w_load = pltpu.make_async_copy(w_hbm.at[pl.ds(half, 64)], w, local_sem.at[0])
    cot_load = pltpu.make_async_copy(cot_hbm, cot, local_sem.at[1])
    mom_load = pltpu.make_async_copy(mom_hbm.at[0], mom, local_sem.at[2])
    tok_loads = []
    for k in range(4):
        cols = pl.ds(pl.multiple_of(xk[k] * 1024, 1024), 1024)
        tok_loads.append(pltpu.make_async_copy(tok_hbm.at[:, cols], tok.at[:, cols], local_sem.at[3 + k]))
    w_load.start()
    cot_load.start()
    for load in tok_loads:
        load.start()
    mom_load.start()
    small = [(kept_hbm, kept_ref), (rows_hbm, rows_ref), (fold_hbm, fold_ref)]
    small = [pltpu.make_async_copy(src, dst, local_sem.at[7 + i]) for i, (src, dst) in enumerate(small)]
    for load in small:
        load.start()

    barrier = pltpu.get_barrier_semaphore()
    everyone = x_peer + z_peer + [y_peer, y_far] + rep_peers
    for peer in everyone:
        pl.semaphore_signal(barrier, inc=1, device_id=peer, device_id_type=MESH)

    used = [0]
    sent = []

    def send(src, dst, peer, tag="rs"):
        n = used[0]
        used[0] += 1
        copy = pltpu.make_async_remote_copy(
            src_ref=src, dst_ref=dst, send_sem=send_sem.at[n], recv_sem=recv_sem.at[n],
            device_id=peer, device_id_type=MESH,
        )
        copy.start()
        sent.append(copy)
        return copy

    def same(view, peer, tag="ag"):
        return send(view, view, peer, tag)

    w_load.wait()
    rows_x, rows_z = pl.ds(half, 32), pl.ds(pl.multiple_of(half + 32, 32), 32)
    rows_c = pl.ds(half, 64)
    wf[x, z, ylo, rows_c] = w[...].astype(BF16)
    pl.semaphore_wait(barrier, len(everyone))
    gx = [same(wf.at[x, z, ylo, rows_x], peer) for peer in x_peer]
    gz = [same(wf.at[x, z, ylo, rows_z], peer) for peer in z_peer]
    far = [(same(wf.at[x, z, ylo, rows_c], y_far, "far"), wf.at[x, z, oy, rows_c])]

    cot_load.wait()
    y1 = []
    for k in range(4):
        xs = xk[k]
        tok_loads[k].wait()

        def block(zz, carry, xs=xs):
            cols = pl.ds(pl.multiple_of((xs * 4 + zz * 2) * 256, 512), 512)
            part = lax.dot_general(
                tok[:, cols], cot[...], FROM_LEFT, preferred_element_type=F32
            ).astype(BF16)
            for p in range(8):
                for q in range(4):
                    chunk = part[q * 128 : q * 128 + 128, p * WIDTH : p * WIDTH + WIDTH]
                    parts[p, xs, zz * 2 + q // 2, q % 2] = chunk
            return carry

        lax.fori_loop(0, 2, block, 0)
        y1.append([send(parts.at[p, xs, :, oy], got_y.at[p, xs], y_peer) for p in Y_PIECES])
        if k == 0:
            for copy in gx + gz:
                copy.wait_recv()
            hx, hz = [None] * 3, [None] * 3
            for i in (1, 2):
                hx[i] = same(wf.at[:, z, ylo, rows_x], z_peer[i])
                hz[i] = same(wf.at[x, :, ylo, rows_z], x_peer[i])
            for i in (1, 2, 0):
                far.append((same(wf.at[xk[i], z, ylo, rows_x], y_far, "far"), wf.at[xk[i], z, oy, rows_x]))
                far.append((same(wf.at[x, zk[i], ylo, rows_z], y_far, "far"), wf.at[x, zk[i], oy, rows_z]))

    def block_of(p, place, h):
        if p in X_PIECES:
            return parts.at[p, place, pl.ds(2 * h, 2)]
        return parts.at[p, pl.ds(2 * h, 2), place]

    def line(p):
        return (x, xk, x_peer) if p in X_PIECES else (z, zk, z_peer)

    s1 = {}

    def start_s1(p):
        _, places, peers = line(p)
        far_place, right, left = places[0], places[1], places[2]
        to_right, to_left = peers[1], peers[2]
        s1[p] = [
            send(block_of(p, far_place, 0), got_s1.at[p - 2, 0], to_right),
            send(block_of(p, far_place, 1), got_s1.at[p - 2, 1], to_left),
            send(block_of(p, right, 1), got_s1.at[p - 2, 2], to_right),
            send(block_of(p, left, 0), got_s1.at[p - 2, 3], to_left),
        ]

    def add_into(ref, sources, count):
        def one(i, carry):
            total = ref(i)[...].astype(F32)
            for source in sources:
                total += source(i)[...].astype(F32)
            ref(i)[...] = total.astype(BF16)
            return carry

        lax.fori_loop(0, count, one, 0, unroll=min(2, count))

    def chunk_of(p, place, h):
        if p in X_PIECES:
            return lambda c: parts.at[p, place, 2 * h + c // 2, c % 2]
        return lambda c: parts.at[p, 2 * h + c // 2, place, c % 2]

    def got(p, slot):
        return lambda c: got_s1.at[p - 2, slot, c // 2, c % 2]

    def pass_on(p):
        _, places, peers = line(p)
        right, left = places[1], places[2]
        s1[p][0].wait_recv()
        add_into(chunk_of(p, right, 0), [got(p, 0)], 4)
        s1[p].append(send(block_of(p, right, 0), got_s1.at[p - 2, 4], peers[1]))
        s1[p][1].wait_recv()
        add_into(chunk_of(p, left, 1), [got(p, 1)], 4)
        s1[p].append(send(block_of(p, left, 1), got_s1.at[p - 2, 5], peers[2]))

    def mine(p, c, y):
        if p in X_PIECES or p == Y_PIECES[0]:
            return parts.at[p, x, c, y]
        return parts.at[p, c, z, y]

    y2, last = {}, {}

    def finish_s1(p):
        place, _, _ = line(p)
        for copy in s1[p][2:]:
            copy.wait_recv()
        add_into(chunk_of(p, place, 0), [got(p, 3), got(p, 4)], 4)
        add_into(chunk_of(p, place, 1), [got(p, 2), got(p, 5)], 4)
        if p in X_PIECES:
            view = parts.at[p, x, :, oy]
        else:
            view = parts.at[p, :, z, oy]
        y2[p] = send(view, got_y2.at[p - 2], y_peer)

    def finish_y(p):
        y2[p].wait_recv()
        add_into(lambda c: mine(p, c, ylo), [lambda c: got_y2.at[p - 2, c]], 4)
        start_last(p)

    def start_last(p):
        peers, places = (z_peer, zk) if p in X_PIECES or p == Y_PIECES[0] else (x_peer, xk)
        last[p] = [send(mine(p, places[k], ylo), got_last.at[p, k], peers[k]) for k in range(3)]

    me = lax.axis_index("rep")

    def prepare():
        mom_load.wait()
        for load in small:
            load.wait()
        numbers[...] = kept_lanes(kept_ref[me])
        ex[me] = jnp.zeros((32, 128), F32)

    def finish(*pieces):
        fields = []
        for p in pieces:
            for copy in last[p]:
                copy.wait_recv()
            total = parts[p, x, z, ylo].astype(F32)
            for k in range(3):
                total += got_last[p, k].astype(F32)
            cols = slice(p * WIDTH, p * WIDTH + WIDTH)
            current = DECAY * mom[:, cols] + total * (1.0 / np.sqrt(24576.0))
            cur[:, cols] = current
            fields.append(current)
        mid = dot_left(rows_ref[...], jnp.concatenate(fields, axis=1))
        mid = jnp.concatenate([mid[:, i * WIDTH : i * WIDTH + WIDTH] for i in range(len(pieces))], axis=0)
        coefs_all = dot_right(mid, rows_ref[...], TURNED)
        places = block_numbers(WIDTH)
        shares = []
        for i, p in enumerate(pieces):
            coefs = coefs_all[i * 128 : i * 128 + 128].reshape(2, 8, 8, WIDTH)
            cols = slice(p * WIDTH, p * WIDTH + WIDTH)
            masks = [
                [
                    places == jnp.broadcast_to(numbers[2 * a + which, cols].reshape(1, 1, WIDTH), (8, 8, WIDTH))
                    for a in range(2)
                ]
                for which in range(2)
            ]
            folded = [
                jnp.sum(jnp.where(masks[which][a], coefs[a], 0.0), axis=0) for which in range(2) for a in range(2)
            ]
            shares.append(dot_marks(jnp.concatenate(folded, axis=0), fold_ref[cols]))
            for a in range(2):
                kept_here = jnp.where(masks[0][a] | masks[1][a], coefs[a], 0.0)
                dense[a * 64 : a * 64 + 64, cols] = kept_here.reshape(64, WIDTH)
        ex[me] += sum(shares[1:], shares[0])

    def input_grad(plane, low, high):
        def one(i, carry):
            xx, zz = i // 2, (i % 2) * 2
            rows = jnp.concatenate([wf[xx, zz, plane], wf[xx, zz + 1, plane]], axis=0)
            out = lax.dot_general(cot[...], rows, TURNED, preferred_element_type=F32).astype(BF16)
            for j in range(2):
                cols = pl.ds(pl.multiple_of(((xx * 4 + zz + j) * 2 + plane) * 128, 128), 128)
                ig[:, cols] = out[:, j * 128 : j * 128 + 128]
            return carry

        lax.fori_loop(low, high, one, 0)

    onward = []
    for i in (1, 2):
        zs, xs = zk[3 - i], xk[3 - i]
        pair = pl.ds(2 * (i - 1), 2)
        hx[i].wait_recv()
        onward.append(same(wf.at[pair, zs, ylo, rows_x], z_peer[i]))
        far.append((same(wf.at[:, zs, ylo, rows_x], y_far, "far"), wf.at[:, zs, oy, rows_x]))
        hz[i].wait_recv()
        onward.append(same(wf.at[xs, pair, ylo, rows_z], x_peer[i]))
        far.append((same(wf.at[xs, :, ylo, rows_z], y_far, "far"), wf.at[xs, :, oy, rows_z]))
    for p in (2, 5, 3, 6):
        start_s1(p)
    pass_on(2)
    pass_on(5)
    start_s1(4)
    start_s1(7)
    for copy in onward:
        copy.wait_recv()
    far.append((same(wf.at[:, zk[0], ylo, rows_x], y_far, "far"), wf.at[:, zk[0], oy, rows_x]))
    far.append((same(wf.at[xk[0], :, ylo, rows_z], y_peer, "far"), wf.at[xk[0], :, oy, rows_z]))
    near = same(wf.at[:, :, ylo, rows_c], core_peer, "near")
    pass_on(3)
    pass_on(6)
    near.wait_recv()
    input_grad(ylo, 0, 8)

    prepare()
    for k in range(4):
        xs = xk[k]
        for p in Y_PIECES:
            y1[k][p].wait_recv()
            add_into(
                lambda c, p=p, xs=xs: parts.at[p, xs, c, ylo], [lambda c, p=p, xs=xs: got_y.at[p, xs, c]], 4
            )
    pass_on(4)
    pass_on(7)
    x2 = [send(parts.at[0, xk[k], :, ylo], got_x2.at[k], x_peer[k]) for k in range(3)]
    z2 = [send(parts.at[1, :, zk[k], ylo], got_z2.at[k], z_peer[k]) for k in range(3)]
    finish_s1(2)
    finish_s1(5)

    def forward(count):
        for copy, view in far[:count]:
            copy.wait_recv()
            near2.append(same(view, core_peer, "far"))
        del far[:count]

    near2 = []
    forward(7)
    finish_s1(3)
    finish_s1(6)
    finish_y(2)
    finish_y(5)
    finish_s1(4)
    finish_s1(7)
    for copy in x2:
        copy.wait_recv()
    add_into(lambda c: mine(0, c, ylo), [lambda c, k=k: got_x2.at[k, c] for k in range(3)], 4)
    start_last(0)
    for copy in z2:
        copy.wait_recv()
    add_into(lambda c: mine(1, c, ylo), [lambda c, k=k: got_z2.at[k, c] for k in range(3)], 4)
    start_last(1)
    finish_y(3)
    finish_y(6)
    forward(6)
    finish(2, 5)
    finish_y(4)
    finish_y(7)
    for copy in near2:
        copy.wait_recv()
    input_grad(oy, 0, 4)
    finish(3, 6)
    finish(0, 1)
    finish(4, 7)
    shared = [same(ex.at[me], peer, "ex") for peer in rep_peers]
    newmom[0] = cur[...] - from_coefs(dense[...], rows_ref[...])

    input_grad(oy, 4, 8)
    for copy in shared:
        copy.wait_recv()
    ex_out[...] = ex[...]
    for copy in sent:
        copy.wait_send()


def last_kernel(
    ig, mom, ex_ref, kept_hbm, w_hbm, rows_hbm, fold_hbm, ones_hbm,
    ig_out, mom_out, neww_out, upd_out,
    w_ref, kept_ref, rows_ref, fold_ref, ones_ref, neww_ref, upd_ref, sem,
):
    small = [(kept_hbm, kept_ref), (fold_hbm, fold_ref), (rows_hbm, rows_ref), (ones_hbm, ones_ref), (w_hbm, w_ref)]
    small = [pltpu.make_async_copy(src, dst, sem.at[7 + i]) for i, (src, dst) in enumerate(small)]
    for load in small:
        load.start()
    stores = [
        pltpu.make_async_copy(ig.at[pl.ds(i * 192, 192)], ig_out.at[pl.ds(i * 192, 192)], sem.at[i]) for i in range(4)
    ]
    stores.append(pltpu.make_async_copy(mom, mom_out, sem.at[4]))
    for store in stores:
        store.start()
    for load in small:
        load.wait()
    total = [jnp.zeros((8, 8, 1024), F32)] * 2
    wide = dot_marks(ex_ref[...].reshape(128, 128), fold_ref[...], TURNED).reshape(4, 2, 2, 8, 1024)
    numbers = kept_lanes(kept_ref[...].reshape(16, 16))
    places = block_numbers(1024)
    for r in range(4):
        for a in range(2):
            value = 0.0
            for which in (1, 0):
                at = r * 4 + a * 2 + which
                mask = places == jnp.broadcast_to(numbers[at : at + 1].reshape(1, 1, 1024), (8, 8, 1024))
                value = jnp.where(mask, jnp.broadcast_to(wide[r, which, a][None], (8, 8, 1024)), value)
            total[a] += value
    field = jnp.concatenate([t.reshape(64, 1024) for t in total], axis=0)
    average = from_coefs(field, rows_ref[...]) * 0.25
    squares = jnp.sum((average * average).reshape(2, 64, 1024), axis=1)
    means = dot_marks(side_by_side(squares, 128), ones_ref[...]) * (1.0 / (TILE * TILE))
    spread = jnp.sqrt(means + 1e-06)
    for i in range(8):
        for a in range(2):
            rows_a, cols = slice(a * 64, a * 64 + 64), slice(i * 128, i * 128 + 128)
            avg = average[rows_a, cols]
            update = avg / (jnp.abs(avg) + spread[i * 2 + a : i * 2 + a + 1])
            upd_ref[rows_a, cols] = update
            neww_ref[rows_a, cols] = w_ref[rows_a, cols] - STEP * update
    results = [(neww_ref, neww_out), (upd_ref, upd_out)]
    results = [pltpu.make_async_copy(src, dst, sem.at[5 + i]) for i, (src, dst) in enumerate(results)]
    for store in results:
        store.start()
    for store in stores + results:
        store.wait()


def body(tokens, cotangent, weight, momentum, kept):
    vmem = pl.BlockSpec(memory_space=pltpu.VMEM)
    any_space = pl.BlockSpec(memory_space=pl.ANY)
    rows, fold = jnp.asarray(two_halves(dct_matrix(2))), jnp.asarray(fold_matrix())
    ones = jnp.asarray(np.kron(np.eye(2), np.ones((TILE, TILE))).astype(jnp.bfloat16))
    kept = kept.transpose(0, 1, 3, 2).reshape(4, 4, 16)
    constants = [
        pltpu.VMEM((4, 4, 16), jnp.int32),
        pltpu.VMEM((2, 128, 128), BF16),
        pltpu.VMEM((1024, 128), BF16),
    ]
    sems = 160
    between = pl.pallas_call(
        main_kernel,
        out_shape=(
            pltpu.VMEM((768, 4096), BF16),
            pltpu.VMEM((1, 128, 1024), F32),
            pltpu.VMEM((4, 32, 128), F32),
        ),
        in_specs=[any_space] * 7,
        out_specs=(vmem, vmem, vmem),
        scratch_shapes=[
            pltpu.VMEM((768, 4096), BF16),
            pltpu.VMEM((768, 1024), BF16),
            pltpu.VMEM((64, 1024), F32),
            pltpu.VMEM((128, 1024), F32),
            *constants,
            pltpu.VMEM((4, 4, 2, 128, 1024), BF16),
            pltpu.VMEM((8, 4, 4, 2, 128, WIDTH), BF16),
            pltpu.VMEM((2, 4, 4, 128, WIDTH), BF16),
            pltpu.VMEM((6, 6, 2, 2, 128, WIDTH), BF16),
            pltpu.VMEM((3, 4, 128, WIDTH), BF16),
            pltpu.VMEM((3, 4, 128, WIDTH), BF16),
            pltpu.VMEM((6, 4, 128, WIDTH), BF16),
            pltpu.VMEM((8, 3, 128, WIDTH), BF16),
            pltpu.VMEM((128, 1024), F32),
            pltpu.VMEM((128, 1024), F32),
            pltpu.VMEM((4, 1024), F32),
            pltpu.VMEM((4, 32, 128), F32),
            pltpu.SemaphoreType.DMA((10,)),
            pltpu.SemaphoreType.DMA((sems,)),
            pltpu.SemaphoreType.DMA((sems,)),
        ],
        compiler_params=pltpu.CompilerParams(
            collective_id=0, has_side_effects=True, vmem_limit_bytes=48 << 20
        ),
        cost_estimate=pl.CostEstimate(flops=13 * 10**9, bytes_accessed=20 * 10**6, transcendentals=0),
        name="gradients",
    )(tokens, cotangent, weight, momentum, kept, rows, fold)
    between = [pltpu.with_memory_space_constraint(a, pltpu.VMEM) for a in between]
    return pl.pallas_call(
        last_kernel,
        out_shape=(
            jax.ShapeDtypeStruct((768, 4096), BF16),
            jax.ShapeDtypeStruct((1, 128, 1024), F32),
            jax.ShapeDtypeStruct((128, 1024), F32),
            jax.ShapeDtypeStruct((128, 1024), F32),
        ),
        in_specs=[vmem] * 3 + [any_space] * 5,
        out_specs=(any_space, any_space, any_space, any_space),
        scratch_shapes=[
            pltpu.VMEM((128, 1024), F32),
            *constants,
            pltpu.VMEM((128, 128), BF16),
            pltpu.VMEM((128, 1024), F32),
            pltpu.VMEM((128, 1024), F32),
            pltpu.SemaphoreType.DMA((12,)),
        ],
        compiler_params=pltpu.CompilerParams(vmem_limit_bytes=40 << 20),
        name="step",
    )(*between, kept, weight, rows, fold, ones)


def solution(mesh):
    in_specs = (
        P(("rep", "fsdp"), None),
        P(("rep", "fsdp"), None),
        P("fsdp", None),
        P("rep", "fsdp", None),
        P(None, "fsdp", None, None),
    )
    out_specs = (P(("rep", "fsdp"), None), P("rep", "fsdp", None), P("fsdp", None), P("fsdp", None))
    return jax.shard_map(body, mesh=mesh, in_specs=in_specs, out_specs=out_specs, check_vma=False)
```
